32 devices in a mesh: wide: 8 (over y, x, core), narrow: 4 (over z).
Axes of the slice: x: 2, y: 2, z: 4, core: 2. Of those that a mesh axis runs over, the one named last changes fastest.
Arguments:
- block_in: bfloat16 [32, 1024, 768], P(('wide', 'narrow')), may hold values from -6 to 6
- seq_lengths: int32 [32], P(('wide', 'narrow')), may hold values from 192 to 1024, as said below
- routes: int32 [32, 1024, 1], P(('wide', 'narrow')), may hold values from 0 to 7; in each aligned block of 1024 rows (0 to 1023, 1024 to 2047, ..., all dimensions but the last counted through in order) at most 192 rows name the same one
- first_gain: float32 [768], replicated, may hold values from 0.1 to 1.9
- first_shift: float32 [768], replicated, may hold values from -3 to 3
- query_weight: bfloat16 [768, 768], replicated, may hold values from -0.21875 to 0.21875
- key_weight: bfloat16 [768, 768], replicated, may hold values from -0.21875 to 0.21875
- value_weight: bfloat16 [768, 768], replicated, may hold values from -0.21875 to 0.21875
- output_weight: bfloat16 [768, 768], replicated, may hold values from -1.75 to 1.75
- second_gain: float32 [768], replicated, may hold values from 0.1 to 1.9
- second_shift: float32 [768], replicated, may hold values from -3 to 3
- centroids: bfloat16 [768, 8], replicated, may hold values from -0.21875 to 0.21875
- hidden_weight: bfloat16 [8, 768, 3072], P('wide', None, 'narrow'), may hold values from -0.21875 to 0.21875
- down_weight: bfloat16 [8, 3072, 768], P('wide', 'narrow'), may hold values from -0.21875 to 0.21875
- cotangent: bfloat16 [32, 1024, 768], P(('wide', 'narrow')), may hold values from -6 to 6
Outputs:
- block_out: bfloat16 [32, 1024, 768], P(('wide', 'narrow'))
- input_grad: bfloat16 [32, 1024, 768], P(('wide', 'narrow'))
- first_gain_grad: float32 [768], replicated
- first_shift_grad: float32 [768], replicated
- query_grad: float32 [768, 768], replicated
- key_grad: float32 [768, 768], replicated
- value_grad: float32 [768, 768], replicated
- output_weight_grad: float32 [768, 768], replicated
- second_gain_grad: float32 [768], replicated
- second_shift_grad: float32 [768], replicated
- centroids_grad: float32 [768, 8], replicated
- hidden_grad: float32 [8, 768, 3072], P('wide', None, 'narrow')
- down_grad: float32 [8, 3072, 768], P('wide', 'narrow')
The draws below stay inside these ranges and needn't reach their ends.
Inputs may be any that keep to these rules, and one draw needn't show every extreme that they name: `seq_lengths`: each sequence's true length; some sequence has all 1024 slots live. `routes`: among the tokens of one device (1 x 1024 consecutive slots, padding included) no expert is named by more than 192 tokens, a bound that some block reaches.
All inputs are finite; a program needn't handle non-finite values.
Results may differ from the reference program's by a relative error of at most 0.015.
Values may be sent and summed in bfloat16 or wider, within the bound.
No kernel may reach another device: no remote copies, remote signals or barrier semaphores. Data moves between devices by JAX's collectives and lax.ppermute only.
A program may use at most 384 MiB of HBM per device.

```python
import math
from functools import partial
import jax
import jax.numpy as jnp
import numpy as np
from jax import lax

D = 768
HEADS = 12
HEAD = 64
FF = 3072
LEN = 1024
SEQ_DEV = 1
EXPERTS = 8
SEQS = 32
CAP = 192
N_WIDE = 8
N_NARROW = 4


def draw_seq_lengths(key, part):
    key = jax.random.fold_in(key, 7)
    first_key, second_key, third_key = jax.random.split(key, 3)
    reach = math.isqrt(LEN * 13 // 16)
    factor_one = jax.random.randint(first_key, (SEQS,), 0, reach + 1)
    factor_two = jax.random.randint(second_key, (SEQS,), 0, reach + 1)
    lengths = LEN - factor_one * factor_two
    chosen = jax.random.randint(third_key, (), 0, SEQS)
    lengths = jnp.where(jnp.arange(SEQS) == chosen, LEN, lengths)
    return lengths.astype(jnp.int32)


def levels(stream_key, extent, shards, low, high):
    def one(position, blocks):
        steps = jax.random.uniform(jax.random.fold_in(jax.random.fold_in(stream_key, 6), position), (blocks,), jnp.float32, low / len(shards), high / len(shards))
        return jnp.repeat(jnp.exp(steps), extent[position] // blocks).reshape((-1,) + (1,) * (len(extent) - position - 1))

    factor_of = one(*shards[0])
    for cut in shards[1:]:
        factor_of = factor_of * one(*cut)
    return factor_of


def shared_out(stream_key, own, number, rows, number_of, top, bound, slope):
    ranking = jax.random.permutation(stream_key, number_of)
    packed, common = load_shares(number_of, rows * top, bound, slope, True), load_shares(number_of, rows * top, bound, slope, False)
    places = jnp.arange(number_of)

    def named(tallies, turn):
        used = int((tallies > 0).sum())
        fixed = max(1, used // 4)
        passed = fixed + (places - fixed + turn * (used - fixed)) % max(1, number_of - fixed)
        return jnp.zeros((number_of,), jnp.int32).at[ranking[jnp.where(places < fixed, places, passed)]].set(jnp.asarray(tallies, jnp.int32))

    tallies = jnp.where(number % 4 == 0, named(packed, number // 4), named(common, number - number // 4 - 1))
    mixed = jax.random.permutation(jax.random.fold_in(own, 3), number_of)
    giver, receiver = mixed[0:number_of // 2 * 2:2], mixed[1:number_of // 2 * 2:2]
    room = jnp.minimum(tallies[giver] - 1, bound - tallies[receiver]) // 2
    room = jnp.where((giver == ranking[0]) | (receiver == ranking[0]) | (tallies[receiver] == 0), 0, jnp.maximum(room, 0))
    passed = jax.random.randint(jax.random.fold_in(own, 4), (number_of // 2,), 0, 1 << 20) % (room + 1)
    tallies = tallies.at[giver].add(-passed).at[receiver].add(passed)
    items = jnp.searchsorted(jnp.cumsum(tallies), jnp.arange(rows * top), side="right").astype(jnp.int32)
    table = items.reshape(top, rows).T
    table = table[jax.random.permutation(jax.random.fold_in(own, 1), rows)]
    turn = jax.random.randint(jax.random.fold_in(own, 2), (rows, 1), 0, top)
    return jnp.take_along_axis(table, (jnp.arange(top)[None, :] + turn) % top, axis=1)


def load_shares(number_of, total, limit, lean, full):
    loads = [(1 << 20) // math.isqrt(standing ** lean) + 1 for standing in range(1, number_of + 1)]
    largest = limit if full else min(limit, max(-(-total // number_of), total * loads[0] // sum(loads)))
    least = 1 if total - largest >= number_of - 1 else 0
    given, spare = [largest] + [least] * (number_of - 1), total - largest - least * (number_of - 1)
    while spare > 0:
        movable = [i for i in range(1, number_of) if given[i] < largest] or [i for i in range(1, number_of) if given[i] < limit]
        mass, remaining = sum([loads[i] for i in movable]), spare
        for i in movable:
            addition = min(limit - given[i], max(1, remaining * loads[i] // mass), spare)
            given[i] = given[i] + addition
            spare = spare - addition
    return np.array(given)


def bell_draw(rng, dims, width, most, cuts=(), kind=jnp.bfloat16):
    loudness = levels(rng, dims, cuts, -0.22, 0.18) if cuts else 1.0
    values = jax.random.normal(rng, dims, jnp.float32) * width * loudness
    return jnp.minimum(jnp.maximum(values, -most), most).astype(kind)


def setup_inputs(seed: int = 0) -> dict:
    key_of = jax.random.split(jax.random.key(seed), 16)
    block_in = bell_draw(key_of[0], (SEQS, LEN, D), 1.0, 6.0, ((0, 32),))
    seq_lengths = draw_seq_lengths(jax.random.fold_in(key_of[15], 71), 0)
    routes_keys = jax.random.split(jax.random.fold_in(key_of[2], 1), SEQS * LEN // (SEQ_DEV * LEN))
    routes_turns = jax.random.permutation(jax.random.fold_in(key_of[2], 3), SEQS * LEN // (SEQ_DEV * LEN))
    routes = jax.vmap(lambda own, number: shared_out(jax.random.fold_in(key_of[2], 2), own, number, SEQ_DEV * LEN, EXPERTS, 1, CAP, 1))(routes_keys, routes_turns).reshape((SEQS, LEN, 1))
    first_gain = jnp.clip(1.0 + 0.18 * jax.random.normal(key_of[3], (D,), jnp.float32), 0.1, 1.9)
    first_shift = bell_draw(key_of[4], (D,), 0.3, 3.0, (), jnp.float32)
    query_weight = bell_draw(key_of[5], (D, D), D ** -0.5, 0.21875)
    key_weight = bell_draw(key_of[6], (D, D), D ** -0.5, 0.21875)
    value_weight = bell_draw(key_of[7], (D, D), D ** -0.5, 0.21875)
    output_weight = bell_draw(key_of[8], (D, D), (D * 16 // LEN) ** -0.5, 1.75)
    second_gain = jnp.clip(1.0 + 0.18 * jax.random.normal(key_of[9], (D,), jnp.float32), 0.1, 1.9)
    second_shift = bell_draw(key_of[10], (D,), 0.3, 3.0, (), jnp.float32)
    centroids = bell_draw(key_of[11], (D, EXPERTS), D ** -0.5, 0.21875)
    hidden_weight = bell_draw(key_of[12], (EXPERTS, D, FF), D ** -0.5, 0.21875, ((0, 8), (2, 4)))
    down_weight = bell_draw(key_of[13], (EXPERTS, FF, D), (FF // 4) ** -0.5, 0.21875, ((0, 8), (1, 4)))
    cotangent = bell_draw(key_of[14], (SEQS, LEN, D), 1.0, 6.0, ((0, 32),))
    return dict(block_in=block_in, seq_lengths=seq_lengths, routes=routes, first_gain=first_gain, first_shift=first_shift, query_weight=query_weight, key_weight=key_weight, value_weight=value_weight, output_weight=output_weight, second_gain=second_gain, second_shift=second_shift, centroids=centroids, hidden_weight=hidden_weight, down_weight=down_weight, cotangent=cotangent)


EPSILON = 1e-05
MASKED_SCORE = -1000000000.0
EXACT = lax.Precision.HIGHEST

@jax.custom_vjp
def low(v):
    return lax.optimization_barrier(v.astype(jnp.bfloat16)).astype(jnp.float32)

@jax.custom_vjp
def low_back(v):
    return v

def low_keep(v):
    return (low(v), None)

def low_pass(kept, grad):
    return (grad,)

def back_keep(v):
    return (v, None)

def back_low(kept, grad):
    return (low(grad),)
low.defvjp(low_keep, low_pass)
low_back.defvjp(back_keep, back_low)

def rounded_both(values):
    return low_back(low(values))

def matmul(left, right):
    return jnp.dot(left, right, precision=EXACT)

def normalize(values, gain, shift):
    centre = lax.optimization_barrier(jnp.mean(values, -1, keepdims=True))
    centered = values - centre
    spread = lax.optimization_barrier(jnp.mean(centered * centered, -1, keepdims=True))
    return centered * lax.rsqrt(spread + EPSILON) * gain + shift

def attend_one(sequence, seq_len, first_gain, first_shift, query_weight, key_weight, value_weight, output_weight):
    normed = low(normalize(sequence, first_gain, first_shift))
    query = rounded_both(matmul(normed, query_weight)).reshape(LEN, HEADS, HEAD)
    keys = rounded_both(matmul(normed, key_weight)).reshape(LEN, HEADS, HEAD)
    values = rounded_both(matmul(normed, value_weight)).reshape(LEN, HEADS, HEAD)
    scores = jnp.einsum('qhd,khd->hqk', query, keys, precision=EXACT) * HEAD ** (-0.5)
    query_pos = lax.broadcasted_iota(jnp.int32, (LEN, LEN), 0)
    key_pos = lax.broadcasted_iota(jnp.int32, (LEN, LEN), 1)
    allowed = (key_pos <= query_pos) & (key_pos < seq_len)
    scores = low_back(jnp.where(allowed[None], scores, MASKED_SCORE))
    probs = low(jax.nn.softmax(scores, axis=-1))
    mixed = rounded_both(jnp.einsum('hqk,khd->qhd', probs, values, precision=EXACT).reshape(LEN, D))
    return low_back(matmul(mixed, output_weight))

def expert_one(triple):
    rows_in, first_w, second_w = triple
    before = low_back(matmul(rows_in, first_w))
    active = low(jax.nn.gelu(before, approximate=False))
    return rounded_both(matmul(active, second_w))

def forward(extras, block_in, first_gain, first_shift, query_weight, key_weight, value_weight, output_weight, second_gain, second_shift, centroids, hidden_weight, down_weight):
    seq_lengths, live_flat, route_flat, index = extras

    def attend_pair(couple):
        return attend_one(couple[0], couple[1], first_gain, first_shift, query_weight, key_weight, value_weight, output_weight)
    attended = lax.map(jax.checkpoint(attend_pair), (block_in, seq_lengths))
    resid = (block_in + attended).reshape(SEQS * LEN, D)
    normed = low(normalize(resid, second_gain, second_shift))
    routed = low_back(normed) * live_flat[:, None]
    buffer = jnp.zeros((EXPERTS * N_WIDE * N_NARROW * CAP, D), jnp.float32).at[index].add(routed)
    results = lax.map(jax.checkpoint(expert_one), (buffer.reshape(EXPERTS, N_WIDE * N_NARROW * CAP, D), hidden_weight, down_weight))
    picked = results.reshape(EXPERTS * N_WIDE * N_NARROW * CAP, D)[index] * live_flat[:, None]
    logits = matmul(normed, centroids)
    chosen = jnp.take_along_axis(logits, route_flat[:, None], 1)[:, 0]
    gate = jax.nn.sigmoid(chosen)
    return (resid + gate[:, None] * picked).reshape(SEQS, LEN, D)

def reference(block_in, seq_lengths, routes, first_gain, first_shift, query_weight, key_weight, value_weight, output_weight, second_gain, second_shift, centroids, hidden_weight, down_weight, cotangent):
    positions = jnp.arange(LEN, dtype=jnp.int32)
    live = positions[None, :] < seq_lengths[:, None]
    live_flat = live.reshape(SEQS * LEN).astype(jnp.float32)
    route_flat = routes.reshape(SEQS * LEN).astype(jnp.int32)
    blocks = N_WIDE * N_NARROW
    expert_ids = jnp.arange(EXPERTS, dtype=jnp.int32)
    hot = ((route_flat[:, None] == expert_ids[None, :]) & live.reshape(SEQS * LEN)[:, None]).astype(jnp.int32)
    hot = hot.reshape(blocks, SEQ_DEV * LEN, EXPERTS)
    earlier = jnp.cumsum(hot, axis=1, dtype=jnp.int32) - hot
    slot = lax.optimization_barrier(jnp.sum(earlier * hot, axis=-1, dtype=jnp.int32)).reshape(SEQS * LEN)
    source = jnp.arange(SEQS * LEN, dtype=jnp.int32) // (SEQ_DEV * LEN)
    index = (route_flat * (blocks * CAP) + source * CAP + slot).astype(jnp.int32)
    extras = (seq_lengths, live_flat, route_flat, index)
    floats = (block_in.astype(jnp.float32), first_gain.astype(jnp.float32), first_shift.astype(jnp.float32), query_weight.astype(jnp.float32), key_weight.astype(jnp.float32), value_weight.astype(jnp.float32), output_weight.astype(jnp.float32), second_gain.astype(jnp.float32), second_shift.astype(jnp.float32), centroids.astype(jnp.float32), hidden_weight.astype(jnp.float32), down_weight.astype(jnp.float32))
    result, backward = jax.vjp(partial(forward, extras), *floats)
    upstream = cotangent.astype(jnp.float32) * live.astype(jnp.float32)[:, :, None]
    grads = backward(upstream)
    return (result.astype(jnp.bfloat16), grads[0].astype(jnp.bfloat16), grads[1], grads[2], grads[3], grads[4], grads[5], grads[6], grads[7], grads[8], grads[9], grads[10], grads[11])
```

```python
import functools
import jax
import jax.numpy as jnp
from jax import lax
from jax.experimental import pallas as pl
from jax.experimental.pallas import tpu as pltpu
from jax.sharding import PartitionSpec as P

F32 = jnp.float32
BF16 = jnp.bfloat16
HEADS = 12
EPSILON = 1e-05
MASKED_SCORE = -1000000000.0
PAIR = 128
QTILE = 256


def dot(left, right):
    return jnp.dot(left, right, preferred_element_type=F32)


def dot_tn(left, right):
    return lax.dot_general(left, right, (((0,), (0,)), ((), ())), preferred_element_type=F32)


def dot_nt(left, right):
    return lax.dot_general(left, right, (((1,), (1,)), ((), ())), preferred_element_type=F32)


def lanes_of(head, shape):
    lane = lax.broadcasted_iota(jnp.int32, shape, 1)
    return (lane >= head * (PAIR // 2)) & (lane < (head + 1) * (PAIR // 2))


def attend_kernel(scale, len_ref, q_ref, k_ref, v_ref, mixed_ref, logsum_ref):
    length = q_ref.shape[0]
    tile = min(QTILE, length)
    seq_len = len_ref[0]
    for at in range(length // tile):
        start, finish = at * tile, (at + 1) * tile
        query = q_ref[start:finish, :] * scale
        keys = k_ref[:finish, :]
        values = v_ref[:finish, :]
        key_pos = lax.broadcasted_iota(jnp.int32, (1, finish), 1)
        bias = jnp.where(key_pos < seq_len, 0.0, MASKED_SCORE)
        row = lax.broadcasted_iota(jnp.int32, (tile, tile), 0)
        col = lax.broadcasted_iota(jnp.int32, (tile, tile), 1)
        mixed = None
        for head in range(2):
            zero = jnp.zeros((), BF16)
            q_head = jnp.where(lanes_of(head, query.shape), query, zero)
            scores = dot_nt(q_head, keys) + bias
            last = jnp.where(col <= row, scores[:, start:], MASKED_SCORE)
            scores = last if start == 0 else jnp.concatenate([scores[:, :start], last], 1)
            highest = jnp.max(scores, 1, keepdims=True)
            expo = jnp.exp(scores - highest)
            total = jnp.sum(expo, 1, keepdims=True)
            v_head = jnp.where(lanes_of(head, values.shape), values, zero)
            part = dot(expo.astype(BF16), v_head) * (1.0 / total)
            mixed = part if mixed is None else mixed + part
            logsum = jnp.broadcast_to(highest + jnp.log(total), (tile, PAIR)).T
            logsum_ref[0, head : head + 1, start:finish] = logsum[:1]
        mixed_ref[start:finish, :] = mixed.astype(BF16)


def attend(projected, seq_lengths, heads, scale):
    length, width3 = projected.shape
    width = width3 // 3
    pairs = width // PAIR
    return pl.pallas_call(
        functools.partial(attend_kernel, scale),
        grid_spec=pltpu.PrefetchScalarGridSpec(
            num_scalar_prefetch=1,
            grid=(pairs,),
            in_specs=[
                pl.BlockSpec((length, PAIR), lambda i, s: (0, i)),
                pl.BlockSpec((length, PAIR), lambda i, s: (0, pairs + i)),
                pl.BlockSpec((length, PAIR), lambda i, s: (0, 2 * pairs + i)),
            ],
            out_specs=[
                pl.BlockSpec((length, PAIR), lambda i, s: (0, i)),
                pl.BlockSpec((1, 8, length), lambda i, s: (i, 0, 0)),
            ],
        ),
        out_shape=[
            jax.ShapeDtypeStruct((length, width), BF16),
            jax.ShapeDtypeStruct((pairs, 8, length), F32),
        ],
        compiler_params=pltpu.CompilerParams(vmem_limit_bytes=48 * 1024 * 1024),
        cost_estimate=pl.CostEstimate(
            flops=4 * length * length * width, bytes_accessed=8 * length * width, transcendentals=0
        ),
        name="attend",
    )(seq_lengths, projected, projected, projected)


def attend_back_kernel(
    scale, count, last, len_ref, q_ref, k_ref, v_ref, g_ref, logsum_ref, normed_ref, wq_ref, wk_ref,
    wv_ref, mixed_ref, attn_ref, *refs,
):
    if last:
        sum_ref, in_ref, gain_ref, resid_ref, weight_ref, out_ref, sums_ref = refs[:7]
        grads, normed_t, grad_normed = refs[7:]
    else:
        weight_ref, grad_normed, grads, normed_t = refs
    length = q_ref.shape[0]
    tile = min(QTILE, length)
    seq_len = len_ref[0]
    step = pl.program_id(0)

    @pl.when(step == 0)
    def _():
        for at in range(length // tile):
            normed_t[:, at * tile : (at + 1) * tile] = normed_ref[at * tile : (at + 1) * tile, :].T
        if last:
            grad_normed[...] = sum_ref[...]
        else:
            grad_normed[...] = jnp.zeros_like(grad_normed)

    @pl.when(step < count)
    def _():
        dk_sum = [None] * (length // tile)
        dv_sum = [None] * (length // tile)
        for at in range(length // tile):
            start, finish = at * tile, (at + 1) * tile
            query = q_ref[start:finish, :] * scale
            grad = g_ref[start:finish, :]
            keys = k_ref[:finish, :]
            values = v_ref[:finish, :]
            key_pos = lax.broadcasted_iota(jnp.int32, (finish, 1), 0)
            bias = jnp.where(key_pos < seq_len, 0.0, MASKED_SCORE)
            row = lax.broadcasted_iota(jnp.int32, (tile, tile), 0)
            col = lax.broadcasted_iota(jnp.int32, (tile, tile), 1)
            grad_query = None
            for head in range(2):
                zero = jnp.zeros((), BF16)
                q_head = jnp.where(lanes_of(head, query.shape), query, zero)
                g_head = jnp.where(lanes_of(head, query.shape), grad, zero)
                k_head = jnp.where(lanes_of(head, keys.shape), keys, zero)
                scores = dot_nt(keys, q_head) + bias
                diagonal = jnp.where(row <= col, scores[start:], MASKED_SCORE)
                scores = (
                    diagonal if start == 0 else jnp.concatenate([scores[:start], diagonal], 0)
                )
                probs = jnp.exp(scores - logsum_ref[0, head : head + 1, start:finish])
                grad_probs = dot_nt(values, g_head)
                product = probs * grad_probs
                centre = jnp.sum(product, 0, keepdims=True)
                grad_scores = (product - probs * centre).astype(BF16)
                dv = dot(probs.astype(BF16), g_head)
                dk = dot(grad_scores, q_head)
                for j in range(at + 1):
                    here = slice(j * tile, (j + 1) * tile)
                    dk_sum[j] = dk[here] if dk_sum[j] is None else dk_sum[j] + dk[here]
                    dv_sum[j] = dv[here] if dv_sum[j] is None else dv_sum[j] + dv[here]
                part = dot_tn(grad_scores, k_head)
                grad_query = part if grad_query is None else grad_query + part
            grads[start:finish, :PAIR] = (grad_query * scale).astype(BF16)
        for j in range(length // tile):
            here = slice(j * tile, (j + 1) * tile)
            grads[here, PAIR : 2 * PAIR] = dk_sum[j].astype(BF16)
            grads[here, 2 * PAIR :] = dv_sum[j].astype(BF16)
        weight_ref[...] = dot(normed_t[...], grads[...])
        weights = jnp.concatenate([wq_ref[...], wk_ref[...], wv_ref[...]], 1)
        for at in range(length // tile):
            here = slice(at * tile, (at + 1) * tile)
            grad_normed[here, :] += dot_nt(grads[here, :], weights)

    @pl.when(step == count)
    def _():
        weight_ref[...] = dot_tn(mixed_ref[...], attn_ref[...])
        if last:
            gain_sum, shift_sum = 0.0, 0.0
            for at in range(length // tile):
                here = slice(at * tile, (at + 1) * tile)
                grad = grad_normed[here, :]
                standard, back_norm = norm_back(in_ref[0, here, :].astype(F32), gain_ref[...], grad)
                out_ref[0, here, :] = (resid_ref[here, :] + back_norm).astype(BF16)
                gain_sum += jnp.sum(grad * standard, 0, keepdims=True)
                shift_sum += jnp.sum(grad, 0, keepdims=True)
            sums_ref[0:1, :] = gain_sum
            sums_ref[1:2, :] = shift_sum
            sums_ref[2:8, :] = jnp.zeros((6, sums_ref.shape[1]), F32)


def attend_back(
    projected, grad_mixed, logsum, seq_lengths, scale, part, count, normed, qkv, mixed, grad_attn,
    *more,
):
    length, width = normed.shape
    pairs = width // PAIR
    first = part * count
    last = part == 1
    block = (length, PAIR)
    columns = 3 * PAIR

    def at(i):
        return first + jnp.minimum(i, count - 1)

    wspec = pl.BlockSpec((width, PAIR), lambda i, s: (0, at(i)))
    wide = jax.ShapeDtypeStruct((length, width), F32)
    weight_shape = jax.ShapeDtypeStruct((width, (count + 1) * columns), F32)
    weight_spec = pl.BlockSpec((width, columns), lambda i, s: (0, i))
    in_specs = [
        pl.BlockSpec(block, lambda i, s: (0, at(i))),
        pl.BlockSpec(block, lambda i, s: (0, pairs + at(i))),
        pl.BlockSpec(block, lambda i, s: (0, 2 * pairs + at(i))),
        pl.BlockSpec(block, lambda i, s: (0, at(i))),
        pl.BlockSpec((1, 8, length), lambda i, s: (at(i), 0, 0)),
        whole((length, width)),
        wspec, wspec, wspec,
        whole((length, width)),
        pl.BlockSpec((length, columns), lambda i, s: (0, part), pipeline_mode=pl.Buffered(1)),
    ]
    scratch = [pltpu.VMEM((length, columns), BF16), pltpu.VMEM((width, length), BF16)]
    if last:
        in_specs += [
            whole((length, width)), whole((1, length, width)), whole((1, width)), whole((length, width)),
        ]
        out_specs = [weight_spec, whole((1, length, width)), whole((8, width))]
        out_shape = [
            weight_shape, jax.ShapeDtypeStruct((1, length, width), BF16),
            jax.ShapeDtypeStruct((8, width), F32),
        ]
        scratch += [pltpu.VMEM((length, width), F32)]
    else:
        out_specs = [weight_spec, whole((length, width))]
        out_shape = [weight_shape, wide]
    return pl.pallas_call(
        functools.partial(attend_back_kernel, scale, count, last),
        grid_spec=pltpu.PrefetchScalarGridSpec(
            num_scalar_prefetch=1,
            grid=(count + 1,),
            in_specs=in_specs,
            out_specs=out_specs,
            scratch_shapes=scratch,
        ),
        out_shape=out_shape,
        compiler_params=pltpu.CompilerParams(vmem_limit_bytes=58 * 1024 * 1024),
        cost_estimate=pl.CostEstimate(
            flops=20 * length * length * count * PAIR,
            bytes_accessed=14 * length * count * PAIR,
            transcendentals=0,
        ),
        name="attend_back",
    )(seq_lengths, projected, projected, projected, grad_mixed, logsum, normed, *qkv, mixed, grad_attn, *more)


ERFC = (0.254829592, -0.284496736, 1.421413741, -1.453152027, 1.061405429)
ERFC_RATE = 0.3275911 * 0.5**0.5
ROWS = 256


def gelu_pair(value):
    size = jnp.abs(value)
    t = 1.0 / (1.0 + ERFC_RATE * size)
    poly = t * (
        ERFC[0] + t * (ERFC[1] + t * (ERFC[2] + t * (ERFC[3] + t * ERFC[4])))
    )
    bell = jnp.exp(-0.5 * value * value)
    tail = 0.5 * poly * bell
    below = jnp.where(value < 0, tail, 1.0 - tail)
    return value * below, below + value * (bell * 0.3989422804014327)


def join_pieces(w_ref, w_all):
    pieces, unused, hidden, unused_width = w_ref.shape
    for p in range(pieces):
        for k in range(2):
            w_all[k, p * hidden : (p + 1) * hidden, :] = w_ref[p, k]


def expert_tile(x, g, w_all, active_ref, pre_ref, at):
    units = w_all.shape[1]
    chunk = units if units <= 512 else 512 if units % 512 == 0 else 384
    for start in range(0, units, chunk):
        cols = slice(start, start + chunk)
        active, slope = gelu_pair(dot_nt(x, w_all[0, cols, :]))
        active_ref[at, cols] = active.astype(BF16)
        pre_ref[at, cols] = (dot_nt(g, w_all[1, cols, :]) * slope).astype(BF16)
    return dot(active_ref[at, :], w_all[1]), dot(pre_ref[at, :], w_all[0])


def expert_first_kernel(
    tiles, x_ref, u_ref, cent_ref, w_ref, out_ref, in_ref, dw_ref, g_ref, xt_ref, gt_ref, gate_ref,
    active, grad_pre, w_all,
):
    rows = x_ref.shape[0]
    step = pl.program_id(0)

    @pl.when(step == 0)
    def _():
        join_pieces(w_ref, w_all)

    @pl.when(step < tiles)
    def _():
        at = pl.ds(pl.multiple_of(step * rows, rows), rows)
        x = x_ref[...]
        chosen = jnp.sum(x.astype(F32) * cent_ref[...], 1, keepdims=True)
        gate = 1.0 / (1.0 + jnp.exp(-chosen))
        gate_ref[...] = gate
        g = (gate * u_ref[...].astype(F32)).astype(BF16)
        g_ref[...] = g
        xt_ref[:, at] = x.T
        gt_ref[:, at] = g.T
        out_ref[...], in_ref[...] = expert_tile(x, g, w_all, active, grad_pre, at)

    @pl.when(step >= tiles)
    def _():
        hidden = dw_ref.shape[3]
        cols = pl.ds(pl.multiple_of((step - tiles) * hidden, hidden), hidden)
        dw_ref[0, 0] = dot(xt_ref[...], grad_pre[:, cols]).astype(BF16)
        dw_ref[0, 1] = dot(gt_ref[...], active[:, cols]).astype(BF16)


def expert_middle_kernel(
    x_ref, g_ref, out_in, in_in, w_ref, out_ref, in_ref, active_ref, pre_ref, w_all
):
    @pl.when(pl.program_id(0) == 0)
    def _():
        join_pieces(w_ref, w_all)

    out, grad_in = expert_tile(x_ref[...], g_ref[...], w_all, active_ref, pre_ref, slice(None))
    out_ref[...] = out_in[...] + out
    in_ref[...] = in_in[...] + grad_in


def expert_last_kernel(
    x_ref, g_ref, u_ref, gate_ref, cent_ref, out_in, in_in, w_ref,
    low_ref, back_ref, cent_grad_ref, active_ref, pre_ref, w_all,
):
    @pl.when(pl.program_id(0) == 0)
    def _():
        join_pieces(w_ref, w_all)
        cent_grad_ref[...] = jnp.zeros_like(cent_grad_ref)

    x = x_ref[...]
    out, grad_in = expert_tile(x, g_ref[...], w_all, active_ref, pre_ref, slice(None))
    low = (out_in[...] + out).astype(BF16)
    low_ref[...] = low
    gate = gate_ref[...]
    chosen = jnp.sum(u_ref[...].astype(F32) * low.astype(F32), 1, keepdims=True)
    chosen = chosen * gate * (1.0 - gate)
    back_ref[...] = (in_in[...] + grad_in + chosen * cent_ref[...]).astype(BF16)
    cent_grad_ref[...] += jnp.sum(chosen * x.astype(F32), 0, keepdims=True)


def expert_weights_kernel(xt_ref, gt_ref, active_one, pre_one, active_two, pre_two, dw_ref):
    grad_pre = jnp.concatenate([pre_one[...], pre_two[...]], 1)
    active = jnp.concatenate([active_one[...], active_two[...]], 1)
    dw_ref[0, 0] = dot(xt_ref[...], grad_pre).astype(BF16)
    dw_ref[0, 1] = dot(gt_ref[...], active).astype(BF16)


def whole(shape):
    return pl.BlockSpec(shape, lambda *i: (0,) * len(shape), pipeline_mode=pl.Buffered(1))


EXPERT_PARAMS = pltpu.CompilerParams(vmem_limit_bytes=58 * 1024 * 1024)


def expert_cost(kind, rows, width, hidden, pieces):
    return pl.CostEstimate(
        flops=2 * kind * rows * width * hidden * pieces,
        bytes_accessed=6 * rows * width * 4,
        transcendentals=0,
    )


def expert_first(x, u, cent, w):
    rows, width = x.shape
    pieces, unused, hidden, unused_width = w.shape
    tile = min(ROWS, rows)
    tiles = rows // tile
    units = pieces * hidden

    def tiled(cols):
        return pl.BlockSpec((tile, cols), lambda i: (jnp.minimum(i, tiles - 1), 0))

    wide = jax.ShapeDtypeStruct((rows, width), F32)
    turned = jax.ShapeDtypeStruct((width, rows), BF16)
    return pl.pallas_call(
        functools.partial(expert_first_kernel, tiles),
        grid=(tiles + pieces,),
        in_specs=[tiled(width), tiled(width), whole((1, width)), whole(w.shape)],
        out_specs=[
            tiled(width), tiled(width),
            pl.BlockSpec((1, 2, width, hidden), lambda i: (jnp.maximum(i - tiles, 0), 0, 0, 0)),
            tiled(width), whole(turned.shape), whole(turned.shape), tiled(1),
        ],
        out_shape=[
            wide, wide, jax.ShapeDtypeStruct((pieces, 2, width, hidden), BF16),
            jax.ShapeDtypeStruct((rows, width), BF16), turned, turned,
            jax.ShapeDtypeStruct((rows, 1), F32),
        ],
        scratch_shapes=[
            pltpu.VMEM((rows, units), BF16), pltpu.VMEM((rows, units), BF16),
            pltpu.VMEM((2, units, width), BF16),
        ],
        compiler_params=EXPERT_PARAMS,
        cost_estimate=expert_cost(6, rows, width, hidden, pieces),
        name="expert_first",
    )(x, u, cent, w)


def expert_middle(x, g, out_sum, in_sum, w):
    rows, width = x.shape
    pieces, unused, hidden, unused_width = w.shape
    tile = min(ROWS, rows)
    units = pieces * hidden

    def tiled(cols):
        return pl.BlockSpec((tile, cols), lambda i: (i, 0))

    wide = jax.ShapeDtypeStruct((rows, width), F32)
    kept = jax.ShapeDtypeStruct((rows, units), BF16)
    return pl.pallas_call(
        expert_middle_kernel,
        grid=(rows // tile,),
        in_specs=[tiled(width)] * 4 + [whole(w.shape)],
        out_specs=[tiled(width), tiled(width), tiled(units), tiled(units)],
        out_shape=[wide, wide, kept, kept],
        scratch_shapes=[pltpu.VMEM((2, units, width), BF16)],
        compiler_params=EXPERT_PARAMS,
        cost_estimate=expert_cost(4, rows, width, hidden, pieces),
        name="expert_middle",
    )(x, g, out_sum, in_sum, w)


def expert_last(x, g, u, gate, cent, out_sum, in_sum, w):
    rows, width = x.shape
    pieces, unused, hidden, unused_width = w.shape
    tile = min(ROWS, rows)
    units = pieces * hidden

    def tiled(cols):
        return pl.BlockSpec((tile, cols), lambda i: (i, 0))

    low = jax.ShapeDtypeStruct((rows, width), BF16)
    kept = jax.ShapeDtypeStruct((rows, units), BF16)
    return pl.pallas_call(
        expert_last_kernel,
        grid=(rows // tile,),
        in_specs=[tiled(width)] * 3
        + [tiled(1), whole((1, width)), tiled(width), tiled(width), whole(w.shape)],
        out_specs=[tiled(width), tiled(width), whole((1, width)), tiled(units), tiled(units)],
        out_shape=[low, low, jax.ShapeDtypeStruct((1, width), F32), kept, kept],
        scratch_shapes=[pltpu.VMEM((2, units, width), BF16)],
        compiler_params=EXPERT_PARAMS,
        cost_estimate=expert_cost(4, rows, width, hidden, pieces),
        name="expert_last",
    )(x, g, u, gate, cent, out_sum, in_sum, w)


def expert_weights(xt, gt, one, two, pieces):
    width, rows = xt.shape
    cols = [pair[0].shape[1] // pieces for pair in (one, two)]
    specs = [pl.BlockSpec((rows, c), lambda i: (0, i)) for c in cols for _ in range(2)]
    shape = (pieces, 2, width, sum(cols))
    return pl.pallas_call(
        expert_weights_kernel,
        grid=(pieces,),
        in_specs=[whole(xt.shape), whole(xt.shape), *specs],
        out_specs=pl.BlockSpec((1, *shape[1:]), lambda i: (i, 0, 0, 0)),
        out_shape=jax.ShapeDtypeStruct(shape, BF16),
        compiler_params=EXPERT_PARAMS,
        cost_estimate=expert_cost(2, rows, width, sum(cols), pieces),
        name="expert_weights",
    )(xt, gt, *one, *two)


def norm_back(values, gain, grad):
    centre = jnp.mean(values, -1, keepdims=True)
    centered = values - centre
    spread = jnp.mean(centered * centered, -1, keepdims=True)
    rate = lax.rsqrt(spread + EPSILON)
    standard = centered * rate
    u = grad * gain
    back = rate * (
        u - jnp.mean(u, -1, keepdims=True) - standard * jnp.mean(u * standard, -1, keepdims=True)
    )
    return standard, back


def combine_back_kernel(
    back_ref, target_ref, resid_ref, cot_ref, gain_ref, weight_ref,
    resid_grad_ref, attn_ref, mixed_grad_ref, sums_ref,
):
    @pl.when(pl.program_id(0) == 0)
    def _():
        sums_ref[...] = jnp.zeros_like(sums_ref)

    target = target_ref[...]
    slots = lax.broadcasted_iota(jnp.int32, (1, back_ref.shape[0]), 1)
    grad = dot((target == slots).astype(BF16), back_ref[...])
    standard, back_norm = norm_back(resid_ref[...], gain_ref[...], grad)
    upstream = jnp.where(target >= 0, cot_ref[...].astype(F32), 0.0)
    grad_resid = upstream + back_norm
    resid_grad_ref[...] = grad_resid
    low = grad_resid.astype(BF16)
    attn_ref[...] = low
    mixed_grad_ref[...] = dot_nt(low, weight_ref[...]).astype(BF16)
    sums_ref[0:1, :] += jnp.sum(grad * standard, 0, keepdims=True)
    sums_ref[1:2, :] += jnp.sum(grad, 0, keepdims=True)


def combine_back(back, target, resid, cot, gain, weight):
    length, width = resid.shape
    tile = min(QTILE, length)
    tiled = pl.BlockSpec((tile, width), lambda i: (i, 0))
    low = jax.ShapeDtypeStruct(resid.shape, BF16)
    return pl.pallas_call(
        combine_back_kernel,
        grid=(length // tile,),
        in_specs=[
            whole(back.shape), pl.BlockSpec((tile, 1), lambda i: (i, 0)), tiled, tiled,
            whole((1, width)), whole(weight.shape),
        ],
        out_specs=[tiled, tiled, tiled, whole((8, width))],
        out_shape=[
            jax.ShapeDtypeStruct(resid.shape, F32), low, low, jax.ShapeDtypeStruct((8, width), F32),
        ],
        compiler_params=EXPERT_PARAMS,
        cost_estimate=pl.CostEstimate(
            flops=2 * length * width * (back.shape[0] + width),
            bytes_accessed=20 * length * width,
            transcendentals=0,
        ),
        name="combine_back",
    )(back, target, resid, cot, gain.reshape(1, width), weight)


def spread_kernel(count, flag_ref, *refs):
    sources, (query_ref, key_ref, value_ref, output_ref) = refs[:8], refs[8:]
    step = pl.program_id(0)
    half = query_ref.shape[0] // 2
    for part in range(2):
        mine, other, mine_more, other_more = sources[4 * part : 4 * part + 4]

        @pl.when((step >= part * count) & (step < (part + 1) * count))
        def _():
            for i, (at, left, right) in enumerate(
                [(query_ref, mine, other), (key_ref, mine, other), (value_ref, mine, other)]
                + [(output_ref, mine_more, other_more)]
            ):
                cols = slice(i * PAIR, (i + 1) * PAIR) if i < 3 else slice(None)
                low, high = left[:, cols].astype(F32), right[:, cols].astype(F32)
                at[:half, :] = jnp.where(flag_ref[0] == 0, low, high)
                at[half:, :] = jnp.where(flag_ref[0] == 0, high, low)


def spread(flag, halves, width):
    pairs = width // PAIR
    count = pairs // 2
    half = width // 2
    operands, specs = [], []
    for part, (mine, other) in enumerate(halves):

        def at(i, part=part):
            return jnp.clip(i - part * count, 0, count - 1)

        operands += [mine, other, mine, other]
        specs += [pl.BlockSpec((half, 3 * PAIR), lambda i, s, at=at: (0, at(i)))] * 2
        specs += [pl.BlockSpec((half, PAIR), lambda i, s, at=at: (0, 3 * count + at(i)))] * 2
    out = jax.ShapeDtypeStruct((width, width), F32)
    return pl.pallas_call(
        functools.partial(spread_kernel, count),
        grid_spec=pltpu.PrefetchScalarGridSpec(
            num_scalar_prefetch=1,
            grid=(pairs,),
            in_specs=specs,
            out_specs=[pl.BlockSpec((width, PAIR), lambda i, s: (0, i))] * 4,
        ),
        out_shape=[out] * 4,
        compiler_params=EXPERT_PARAMS,
        name="spread",
    )(flag, *operands)


def normalize(values, gain, shift):
    centre = jnp.mean(values, -1, keepdims=True)
    centered = values - centre
    spread = jnp.mean(centered * centered, -1, keepdims=True)
    return centered * lax.rsqrt(spread + EPSILON) * gain + shift


def xor_pairs(size, flip):
    return [(i, i ^ flip) for i in range(size)]


def exchange(rows, blocks):
    shape = rows.shape
    return lax.all_to_all(
        rows.reshape(blocks, -1, shape[1]), "wide", split_axis=0, concat_axis=0, tiled=True
    ).reshape(shape)


def reduce_halves(parts, sizes, bits):
    flags = []
    for axis, flip in bits:
        flag = (lax.axis_index(axis) // flip) % 2
        half = parts[0].shape[0] // 2
        mine = [lax.dynamic_slice_in_dim(p, flag * half, half, 0) for p in parts]
        theirs = [lax.dynamic_slice_in_dim(p, (1 - flag) * half, half, 0) for p in parts]
        if len(parts) > 1:
            mine, theirs = [jnp.concatenate(mine, 1)], [jnp.concatenate(theirs, 1)]
        came = lax.ppermute(theirs[0].astype(BF16), axis, xor_pairs(sizes[axis], flip))
        parts = [mine[0] + came.astype(F32)]
        flags.append(flag)
    return parts[0].astype(BF16), flags


def gather_halves(total, flags, sizes, bits, stop):
    for at in reversed(range(stop, len(bits))):
        axis, flip = bits[at]
        other = lax.ppermute(total, axis, xor_pairs(sizes[axis], flip))
        if at == 0:
            return total, other
        total = jnp.where(
            flags[at] == 0, jnp.concatenate([total, other], 0), jnp.concatenate([other, total], 0)
        )
    return total


def make_shards(n_wide, n_narrow):
    sizes = {"wide": n_wide, "narrow": n_narrow}
    wide_bits = [("wide", 1 << i) for i in range(n_wide.bit_length() - 1)]
    narrow_bits = [("narrow", 1 << i) for i in range(n_narrow.bit_length() - 1)]
    orders = [
        wide_bits + narrow_bits,
        wide_bits[:1] + wide_bits[2:] + wide_bits[1:2] + narrow_bits,
    ]

    def shards(
        block_in,
        seq_lengths,
        routes,
        first_gain,
        first_shift,
        query_weight,
        key_weight,
        value_weight,
        output_weight,
        second_gain,
        second_shift,
        centroids,
        hidden_weight,
        down_weight,
        cotangent,
    ):
        seqs_here, length, width = block_in.shape
        head_size = width // HEADS
        scale = head_size ** (-0.5)
        tokens = seqs_here * length
        experts_all = centroids.shape[1]
        capacity = 3 * tokens // (2 * experts_all)
        wide_here = lax.axis_index("wide")
        hidden_size = hidden_weight.shape[2]

        third = max(hidden_size // 6 // 128 * 128, 128)
        second = max(hidden_size // 3 // 128 * 128, 128)
        cuts = (0, hidden_size - second - third, hidden_size - third, hidden_size)
        hidden_t = hidden_weight[0].T
        packs = [
            jnp.stack([hidden_t[a:b], down_weight[0, a:b]], 0)[None]
            for a, b in zip(cuts, cuts[1:])
        ]
        weights = [lax.all_gather(pack, "narrow", axis=0, tiled=True) for pack in packs]

        live = lax.broadcasted_iota(jnp.int32, (tokens,), 0) < seq_lengths[0]
        route = routes.reshape(tokens)
        expert_ids = lax.broadcasted_iota(jnp.int32, (tokens, experts_all), 1)
        picked = route[:, None] == expert_ids
        ones_live = (picked & live[:, None]).astype(jnp.int32)
        earlier = jnp.cumsum(ones_live, 0, dtype=jnp.int32) - ones_live
        slot = jnp.sum(earlier * ones_live, 1, dtype=jnp.int32)
        target = route * capacity + slot
        slot_ids = lax.broadcasted_iota(jnp.int32, (tokens, experts_all * capacity), 1)
        target = jnp.where(live, target, -1)[:, None]
        table = (target == slot_ids).astype(BF16)
        cot = cotangent.reshape(tokens, width)

        def to_slots(rows):
            return dot_tn(table, rows).astype(BF16)

        upstream_slots, block_in, *packs = lax.optimization_barrier(
            (to_slots(cot), block_in, *packs)
        )
        upstream_rows = exchange(upstream_slots, experts_all)

        qkv_weight = jnp.concatenate([query_weight, key_weight, value_weight], 1)
        inputs_wide = block_in.reshape(tokens, width).astype(F32)
        normed_low = normalize(inputs_wide, first_gain, first_shift).astype(BF16)
        projected = dot(normed_low, qkv_weight).astype(BF16)
        mixed, logsum = attend(projected, seq_lengths, HEADS, scale)
        mixed, upstream_rows = lax.optimization_barrier((mixed, upstream_rows))
        resid = inputs_wide + dot(mixed, output_weight)
        normed_second = normalize(resid, second_gain, second_shift).astype(BF16)

        rows = exchange(to_slots(normed_second), experts_all)
        own_centroid = lax.dynamic_slice_in_dim(centroids.T, wide_here, 1, 0).astype(F32)
        out_sum, in_sum, weight_grads, grad_rows, rows_t, grad_rows_t, row_gate = expert_first(
            rows, upstream_rows, own_centroid, weights[0]
        )
        out_sum, in_sum, *kept_one = expert_middle(rows, grad_rows, out_sum, in_sum, weights[1])
        out_low, back_rows, own_centroid_grad, *kept_two = expert_last(
            rows, grad_rows, upstream_rows, row_gate, own_centroid, out_sum, in_sum, weights[2]
        )
        back = exchange(back_rows, experts_all)
        more_weight_grads = expert_weights(rows_t, grad_rows_t, kept_one, kept_two, n_narrow)
        grad_resid, grad_attn, grad_mixed, second_sums = combine_back(
            back, target, resid, cot, second_gain, output_weight
        )
        out_low, more_weight_grads, grad_mixed = lax.optimization_barrier(
            (out_low, more_weight_grads, grad_mixed)
        )
        returned = exchange(out_low, experts_all)

        qkv = (query_weight, key_weight, value_weight)
        count = width // PAIR // 2
        shared = (normed_low, qkv, mixed, grad_attn)
        part_one, grad_normed = attend_back(
            projected, grad_mixed, logsum, seq_lengths, scale, 0, count, *shared
        )
        grad_normed, returned = lax.optimization_barrier((grad_normed, returned))
        part_two, input_grad, first_sums = attend_back(
            projected, grad_mixed, logsum, seq_lengths, scale, 1, count, *shared,
            grad_normed, block_in, first_gain.reshape(1, width), grad_resid,
        )
        own_column = expert_ids[:1].reshape(experts_all, 1) == wide_here
        small = jnp.concatenate(
            [jnp.where(own_column, own_centroid_grad, 0.0), second_sums[:2], first_sums[:2]], 0
        )
        small = jnp.pad(small, ((0, -small.shape[0] % 128), (0, 0))).T
        expert_rows_here = dot(table, returned)
        logits = dot(normed_second, centroids)
        gate = jax.nn.sigmoid(jnp.sum(jnp.where(picked, logits, 0.0), 1, keepdims=True))
        block_out = (resid + gate * expert_rows_here).astype(BF16).reshape(block_in.shape)

        first_summed = lax.psum_scatter(weight_grads, "narrow", scatter_dimension=0, tiled=True)
        last_summed = lax.psum_scatter(more_weight_grads, "narrow", scatter_dimension=0, tiled=True)
        summed = [first_summed[0], last_summed[0]]
        hidden_grad = jnp.concatenate([s[0] for s in summed], 1).astype(F32)[None]
        down_grad = jnp.concatenate([s[1] for s in summed], 1).T.astype(F32)[None]

        totals = [
            reduce_halves(parts, sizes, order)
            for parts, order in zip(([part_one], [part_two, small]), orders)
        ]
        flag = totals[0][1][0]
        near = [
            gather_halves(total, flags, sizes, order, len(order) - len(narrow_bits))
            for (total, flags), order in zip(totals, orders)
        ]
        near[0], block_out = lax.optimization_barrier((near[0], block_out))
        near[1], hidden_grad, down_grad = lax.optimization_barrier((near[1], hidden_grad, down_grad))
        halves = [
            gather_halves(total, flags, sizes, order[: len(order) - len(narrow_bits)], 0)
            for total, (unused_total, flags), order in zip(near, totals, orders)
        ]
        query_grad, key_grad, value_grad, output_weight_grad = spread(
            flag.reshape(1), halves, width
        )
        low, high = [h[:, part_two.shape[1] :].astype(F32) for h in halves[1]]
        small = jnp.where(flag == 0, jnp.concatenate([low, high], 0), jnp.concatenate([high, low], 0))
        centroids_grad = small[:, :experts_all]
        second_gain_grad, second_shift_grad, first_gain_grad, first_shift_grad = [
            small[:, experts_all + i] for i in range(4)
        ]

        return (
            block_out,
            input_grad,
            first_gain_grad,
            first_shift_grad,
            query_grad,
            key_grad,
            value_grad,
            output_weight_grad,
            second_gain_grad,
            second_shift_grad,
            centroids_grad,
            hidden_grad,
            down_grad,
        )

    return shards


def solution(mesh):
    tokens_spec = P(("wide", "narrow"), None, None)
    in_specs = (
        tokens_spec,
        P(("wide", "narrow")),
        tokens_spec,
        *[P()] * 9,
        P("wide", None, "narrow"),
        P("wide", "narrow", None),
        tokens_spec,
    )
    out_specs = (
        tokens_spec,
        tokens_spec,
        *[P()] * 9,
        P("wide", None, "narrow"),
        P("wide", "narrow", None),
    )
    return jax.shard_map(
        make_shards(mesh.shape["wide"], mesh.shape["narrow"]),
        mesh=mesh,
        in_specs=in_specs,
        out_specs=out_specs,
        check_vma=False,
    )
```

```python
import functools
import jax
import jax.numpy as jnp
from jax import lax
from jax.experimental import pallas as pl
from jax.experimental.pallas import tpu as pltpu
from jax.sharding import PartitionSpec as P

F32 = jnp.float32
BF16 = jnp.bfloat16
HEADS = 12
EPSILON = 1e-05
MASKED_SCORE = -1000000000.0
PAIR = 128
QTILE = 256


def dot(left, right):
    return jnp.dot(left, right, preferred_element_type=F32)


def dot_tn(left, right):
    return lax.dot_general(left, right, (((0,), (0,)), ((), ())), preferred_element_type=F32)


def dot_nt(left, right):
    return lax.dot_general(left, right, (((1,), (1,)), ((), ())), preferred_element_type=F32)


def lanes_of(head, shape):
    lane = lax.broadcasted_iota(jnp.int32, shape, 1)
    return (lane >= head * (PAIR // 2)) & (lane < (head + 1) * (PAIR // 2))


def packed_rows(length, tile):
    return [sum(range(1, at + 1)) * tile for at in range(length // tile + 1)]


def attend_kernel(scale, len_ref, q_ref, k_ref, v_ref, mixed_ref, probs_ref):
    length = q_ref.shape[0]
    tile = min(QTILE, length)
    seq_len = len_ref[0]
    starts = packed_rows(length, tile)
    for at in range(length // tile):
        start, finish = at * tile, (at + 1) * tile
        query = q_ref[start:finish, :] * scale
        keys = k_ref[:finish, :]
        values = v_ref[:finish, :]
        key_pos = lax.broadcasted_iota(jnp.int32, (finish, 1), 0)
        bias = jnp.where(key_pos < seq_len, 0.0, MASKED_SCORE)
        row = lax.broadcasted_iota(jnp.int32, (tile, tile), 0)
        col = lax.broadcasted_iota(jnp.int32, (tile, tile), 1)
        mixed = None
        for head in range(2):
            zero = jnp.zeros((), BF16)
            q_head = jnp.where(lanes_of(head, query.shape), query, zero)
            scores = dot_nt(keys, q_head) + bias
            diagonal = jnp.where(row <= col, scores[start:], MASKED_SCORE)
            scores = diagonal if start == 0 else jnp.concatenate([scores[:start], diagonal], 0)
            expo = jnp.exp(scores - jnp.max(scores, 0, keepdims=True))
            probs = (expo * (1.0 / jnp.sum(expo, 0, keepdims=True))).astype(BF16)
            probs_ref[0, head, starts[at] : starts[at + 1], :] = probs
            v_head = jnp.where(lanes_of(head, values.shape), values, zero)
            part = dot_tn(probs, v_head)
            mixed = part if mixed is None else mixed + part
        mixed_ref[start:finish, :] = mixed.astype(BF16)


def attend(projected, seq_lengths, scale):
    length, width3 = projected.shape
    width = width3 // 3
    pairs = width // PAIR
    tile = min(QTILE, length)
    rows = packed_rows(length, tile)[-1]
    return pl.pallas_call(
        functools.partial(attend_kernel, scale),
        grid_spec=pltpu.PrefetchScalarGridSpec(
            num_scalar_prefetch=1,
            grid=(pairs,),
            in_specs=[
                pl.BlockSpec((length, PAIR), lambda i, s: (0, i)),
                pl.BlockSpec((length, PAIR), lambda i, s: (0, pairs + i)),
                pl.BlockSpec((length, PAIR), lambda i, s: (0, 2 * pairs + i)),
            ],
            out_specs=[
                pl.BlockSpec((length, PAIR), lambda i, s: (0, i)),
                pl.BlockSpec((1, 2, rows, tile), lambda i, s: (i, 0, 0, 0)),
            ],
        ),
        out_shape=[
            jax.ShapeDtypeStruct((length, width), BF16),
            jax.ShapeDtypeStruct((pairs, 2, rows, tile), BF16),
        ],
        compiler_params=pltpu.CompilerParams(vmem_limit_bytes=48 * 1024 * 1024),
        cost_estimate=pl.CostEstimate(
            flops=4 * length * length * width, bytes_accessed=8 * length * width, transcendentals=0
        ),
        name="attend",
    )(seq_lengths, projected, projected, projected)


def attend_back_kernel(
    scale, counts, part, flag_ref, q_ref, k_ref, v_ref, g_ref, probs_ref, normed_t, *refs
):
    parts = len(counts)
    count = counts[part]
    last = part == parts - 1
    if part == 0:
        mixed_t, attn_ref, mine_ref, theirs_ref, grads = refs
    elif last:
        befores, refs = refs[: parts - 1], refs[parts - 1 :]
        qkv, (in_ref, gain_ref, resid_ref, cent_ref, sums_ref) = refs[:3], refs[3:8]
        mine_ref, theirs_ref, out_ref, grads, sums_scratch = refs[10:]
    else:
        mine_ref, theirs_ref, grads = refs
    length = q_ref.shape[0]
    tile = min(QTILE, length)
    starts = packed_rows(length, tile)
    step = pl.program_id(0)
    half = mine_ref.shape[0]
    columns = 3 * PAIR

    def give(product):
        low, high = product[:half], product[half:]
        mine_ref[...] = jnp.where(flag_ref[0] == 0, low, high)
        theirs_ref[...] = jnp.where(flag_ref[0] == 0, high, low).astype(BF16)

    def pair():
        dk_sum = [None] * (length // tile)
        dv_sum = [None] * (length // tile)
        dq = []
        for at in range(length // tile):
            start, finish = at * tile, (at + 1) * tile
            query = q_ref[start:finish, :] * scale
            grad = g_ref[start:finish, :]
            keys = k_ref[:finish, :]
            values = v_ref[:finish, :]
            grad_query = None
            for head in range(2):
                zero = jnp.zeros((), BF16)
                q_head = jnp.where(lanes_of(head, query.shape), query, zero)
                g_head = jnp.where(lanes_of(head, query.shape), grad, zero)
                k_head = jnp.where(lanes_of(head, keys.shape), keys, zero)
                low = probs_ref[0, head, starts[at] : starts[at + 1], :]
                probs = low.astype(F32)
                product = probs * dot_nt(values, g_head)
                centre = jnp.sum(product, 0, keepdims=True)
                grad_scores = (product - probs * centre).astype(BF16)
                dv = dot(low, g_head)
                dk = dot(grad_scores, q_head)
                for j in range(at + 1):
                    here = slice(j * tile, (j + 1) * tile)
                    dk_sum[j] = dk[here] if dk_sum[j] is None else dk_sum[j] + dk[here]
                    dv_sum[j] = dv[here] if dv_sum[j] is None else dv_sum[j] + dv[here]
                share = dot_tn(grad_scores, k_head)
                grad_query = share if grad_query is None else grad_query + share
            dq.append((grad_query * scale).astype(BF16))
        sides = [dq, [x.astype(BF16) for x in dk_sum], [x.astype(BF16) for x in dv_sum]]
        return jnp.concatenate([jnp.concatenate(side, 0) for side in sides], 1)

    @pl.when(step < count)
    def _():
        found = pair()
        for k in range(3):
            cols = pl.ds(pl.multiple_of(step * PAIR, PAIR), PAIR) if last else slice(None)
            grads[k, :, cols] = found[:, k * PAIR : (k + 1) * PAIR]
        give(dot(normed_t[...], found))

    if part == 0:

        @pl.when(step >= count)
        def _():
            give(dot(mixed_t[...], attn_ref[...]))

    if last:

        @pl.when(step == count)
        def _():
            sums_scratch[...] = jnp.zeros_like(sums_scratch)

        @pl.when(step >= count)
        def _():
            here = pl.ds(pl.multiple_of((step - count) * tile, tile), tile)
            grad = None
            for j in range(parts):
                before = sum(counts[:j])
                cols = slice(before * PAIR, (before + counts[j]) * PAIR)
                for k, weight in enumerate(qkv):
                    side = grads[k, here, :] if j == parts - 1 else befores[j][k]
                    share = dot_nt(side, weight[:, cols])
                    grad = share if grad is None else grad + share
            standard, back_norm = norm_back(in_ref[0].astype(F32), gain_ref[...], grad)
            out_ref[0] = (resid_ref[...] + back_norm).astype(BF16)
            sums_scratch[0:1, :] += jnp.sum(grad * standard, 0, keepdims=True)
            sums_scratch[1:2, :] += jnp.sum(grad, 0, keepdims=True)

        @pl.when(step == count + length // tile - 1)
        def _():
            sums = cent_ref[...]
            rows, width = sums.shape
            place = lax.broadcasted_iota(jnp.int32, (rows, 1), 0)
            for row, ref, k in (
                (rows - 4, sums_ref, 0), (rows - 3, sums_ref, 1),
                (rows - 2, sums_scratch, 0), (rows - 1, sums_scratch, 1),
            ):
                sums = jnp.where(place == row, ref[k : k + 1, :], sums)
            turned = jnp.concatenate([sums, jnp.zeros((PAIR - rows, width), F32)], 0).T
            low, high = turned[:half], turned[half:]
            mine_ref[:, :PAIR] = jnp.where(flag_ref[0] == 0, low, high)
            theirs_ref[:, :PAIR] = jnp.where(flag_ref[0] == 0, high, low).astype(BF16)


def attend_back(flag, projected, grad_mixed, probs, scale, counts, part, normed_t, *more):
    width, length = normed_t.shape
    pairs = width // PAIR
    count = counts[part]
    first = sum(counts[:part])
    last = part == len(counts) - 1
    block = (length, PAIR)
    columns = 3 * PAIR
    extra = width // columns if part == 0 else 0

    def at(i):
        return first + jnp.minimum(i, count - 1)

    own = (count + extra) * columns
    held = own if part == 0 else sum(counts[1:]) * columns + PAIR
    offset = sum(counts[1:part])
    steps = count + (1 if last else extra)
    half_spec = pl.BlockSpec(
        (width // 2, columns), lambda i, s: (0, offset + jnp.minimum(i, steps - 1))
    )
    half_shape = (width // 2, held)
    in_specs = [
        pl.BlockSpec(block, lambda i, s: (0, at(i))),
        pl.BlockSpec(block, lambda i, s: (0, pairs + at(i))),
        pl.BlockSpec(block, lambda i, s: (0, 2 * pairs + at(i))),
        pl.BlockSpec(block, lambda i, s: (0, at(i))),
        pl.BlockSpec((1, *probs.shape[1:]), lambda i, s: (at(i), 0, 0, 0)),
        whole(normed_t.shape),
    ]
    out_specs = [half_spec, half_spec]
    out_shape = [jax.ShapeDtypeStruct(half_shape, F32), jax.ShapeDtypeStruct(half_shape, BF16)]
    scratch = []
    aliases = {}
    if last:
        tile = min(QTILE, length)

        def row(i):
            return jnp.maximum(i - count, 0)

        in_specs += [
            pl.BlockSpec((3, tile, c * PAIR), lambda i, s: (0, row(i), 0)) for c in counts[:-1]
        ]
        in_specs += [whole((width, width))] * 3
        in_specs += [
            pl.BlockSpec((1, tile, width), lambda i, s: (0, row(i), 0)), whole((1, width)),
            pl.BlockSpec((tile, width), lambda i, s: (row(i), 0)), whole(more[-4].shape),
            whole(more[-3].shape),
        ]
        in_specs += [pl.BlockSpec(memory_space=pl.ANY)] * 2
        aliases = {5 + len(more): 0, 6 + len(more): 1}
        extra = length // tile
        out_specs += [pl.BlockSpec((1, tile, width), lambda i, s: (0, row(i), 0))]
        out_shape += [jax.ShapeDtypeStruct((1, length, width), BF16)]
        scratch += [pltpu.VMEM((3, length, count * PAIR), BF16), pltpu.VMEM((8, width), F32)]
    else:
        if part == 0:
            in_specs += [
                whole((width, length)),
                pl.BlockSpec((length, columns), lambda i, s: (0, jnp.maximum(i - count, 0))),
            ]
        out_specs += [
            pl.BlockSpec((3, length, PAIR), lambda i, s: (0, 0, jnp.minimum(i, count - 1)))
        ]
        out_shape += [jax.ShapeDtypeStruct((3, length, count * PAIR), BF16)]
    return pl.pallas_call(
        functools.partial(attend_back_kernel, scale, counts, part),
        grid_spec=pltpu.PrefetchScalarGridSpec(
            num_scalar_prefetch=1,
            grid=(count + extra,),
            in_specs=in_specs,
            out_specs=out_specs,
            scratch_shapes=scratch,
        ),
        out_shape=out_shape,
        input_output_aliases=aliases,
        compiler_params=pltpu.CompilerParams(vmem_limit_bytes=58 * 1024 * 1024),
        cost_estimate=pl.CostEstimate(
            flops=20 * length * length * count * PAIR,
            bytes_accessed=14 * length * count * PAIR,
            transcendentals=0,
        ),
        name="attend_back",
    )(flag, projected, projected, projected, grad_mixed, probs, normed_t, *more)


ERFC = (0.254829592, -0.284496736, 1.421413741, -1.453152027, 1.061405429)
ERFC_RATE = 0.3275911 * 0.5**0.5
ROWS = 256


def gelu_pair(value):
    size = jnp.abs(value)
    t = 1.0 / (1.0 + ERFC_RATE * size)
    poly = t * (
        ERFC[0] + t * (ERFC[1] + t * (ERFC[2] + t * (ERFC[3] + t * ERFC[4])))
    )
    bell = jnp.exp(-0.5 * value * value)
    tail = 0.5 * poly * bell
    below = jnp.where(value < 0, tail, 1.0 - tail)
    return value * below, below + value * (bell * 0.3989422804014327)


def join_pieces(w_ref, w_all):
    pieces, unused, hidden, unused_width = w_ref.shape
    for p in range(pieces):
        for k in range(2):
            w_all[k, p * hidden : (p + 1) * hidden, :] = w_ref[p, k]


def expert_tile(x, g, w_all, active_ref, pre_ref, at):
    units = w_all.shape[1]
    chunk = units if units <= 512 else 512 if units % 512 == 0 else 384
    for start in range(0, units, chunk):
        cols = slice(start, start + chunk)
        active, slope = gelu_pair(dot_nt(x, w_all[0, cols, :]))
        active_ref[at, cols] = active.astype(BF16)
        pre_ref[at, cols] = (dot_nt(g, w_all[1, cols, :]) * slope).astype(BF16)
    return dot(active_ref[at, :], w_all[1]), dot(pre_ref[at, :], w_all[0])


def expert_first_kernel(
    tiles, x_ref, u_ref, cent_ref, w_ref, out_ref, in_ref, dw_ref, g_ref, xt_ref, gt_ref, gate_ref,
    active, grad_pre, w_all,
):
    rows = x_ref.shape[0]
    step = pl.program_id(0)

    @pl.when(step == 0)
    def _():
        join_pieces(w_ref, w_all)

    @pl.when(step < tiles)
    def _():
        at = pl.ds(pl.multiple_of(step * rows, rows), rows)
        x = x_ref[...]
        chosen = jnp.sum(x.astype(F32) * cent_ref[...], 1, keepdims=True)
        gate = 1.0 / (1.0 + jnp.exp(-chosen))
        gate_ref[...] = gate
        g = (gate * u_ref[...].astype(F32)).astype(BF16)
        g_ref[...] = g
        xt_ref[:, at] = x.T
        gt_ref[:, at] = g.T
        out_ref[...], in_ref[...] = expert_tile(x, g, w_all, active, grad_pre, at)

    @pl.when(step >= tiles)
    def _():
        hidden = dw_ref.shape[3]
        cols = pl.ds(pl.multiple_of((step - tiles) * hidden, hidden), hidden)
        dw_ref[0, 0] = dot(xt_ref[...], grad_pre[:, cols]).astype(BF16)
        dw_ref[0, 1] = dot(gt_ref[...], active[:, cols]).astype(BF16)


def expert_last_kernel(
    x_ref, g_ref, u_ref, gate_ref, cent_ref, out_in, in_in, w_ref,
    low_ref, back_ref, cent_grad_ref, active_ref, pre_ref, w_all,
):
    @pl.when(pl.program_id(0) == 0)
    def _():
        join_pieces(w_ref, w_all)
        cent_grad_ref[...] = jnp.zeros_like(cent_grad_ref)

    x = x_ref[...]
    out, grad_in = expert_tile(x, g_ref[...], w_all, active_ref, pre_ref, slice(None))
    low = (out_in[...] + out).astype(BF16)
    low_ref[...] = low
    gate = gate_ref[...]
    chosen = jnp.sum(u_ref[...].astype(F32) * low.astype(F32), 1, keepdims=True)
    chosen = chosen * gate * (1.0 - gate)
    back_ref[...] = (in_in[...] + grad_in + chosen * cent_ref[...]).astype(BF16)
    cent_grad_ref[...] += jnp.sum(chosen * x.astype(F32), 0, keepdims=True)


def expert_weights_kernel(xt_ref, gt_ref, active_ref, pre_ref, dw_ref):
    dw_ref[0, 0] = dot(xt_ref[...], pre_ref[...]).astype(BF16)
    dw_ref[0, 1] = dot(gt_ref[...], active_ref[...]).astype(BF16)


def whole(shape):
    return pl.BlockSpec(shape, lambda *i: (0,) * len(shape), pipeline_mode=pl.Buffered(1))


EXPERT_PARAMS = pltpu.CompilerParams(vmem_limit_bytes=58 * 1024 * 1024)


def expert_cost(kind, rows, width, hidden, pieces):
    return pl.CostEstimate(
        flops=2 * kind * rows * width * hidden * pieces,
        bytes_accessed=6 * rows * width * 4,
        transcendentals=0,
    )


def expert_first(x, u, cent, w):
    rows, width = x.shape
    pieces, unused, hidden, unused_width = w.shape
    tile = min(ROWS, rows)
    tiles = rows // tile
    units = pieces * hidden

    def tiled(cols):
        return pl.BlockSpec((tile, cols), lambda i: (jnp.minimum(i, tiles - 1), 0))

    wide = jax.ShapeDtypeStruct((rows, width), F32)
    turned = jax.ShapeDtypeStruct((width, rows), BF16)
    return pl.pallas_call(
        functools.partial(expert_first_kernel, tiles),
        grid=(tiles + pieces,),
        in_specs=[tiled(width), tiled(width), whole((1, width)), whole(w.shape)],
        out_specs=[
            tiled(width), tiled(width),
            pl.BlockSpec((1, 2, width, hidden), lambda i: (jnp.maximum(i - tiles, 0), 0, 0, 0)),
            tiled(width), whole(turned.shape), whole(turned.shape), tiled(1),
        ],
        out_shape=[
            wide, wide, jax.ShapeDtypeStruct((pieces, 2, width, hidden), BF16),
            jax.ShapeDtypeStruct((rows, width), BF16), turned, turned,
            jax.ShapeDtypeStruct((rows, 1), F32),
        ],
        scratch_shapes=[
            pltpu.VMEM((rows, units), BF16), pltpu.VMEM((rows, units), BF16),
            pltpu.VMEM((2, units, width), BF16),
        ],
        compiler_params=EXPERT_PARAMS,
        cost_estimate=expert_cost(6, rows, width, hidden, pieces),
        name="expert_first",
    )(x, u, cent, w)


def expert_last(x, g, u, gate, cent, out_sum, in_sum, w):
    rows, width = x.shape
    pieces, unused, hidden, unused_width = w.shape
    tile = min(ROWS, rows)
    units = pieces * hidden

    def tiled(cols):
        return pl.BlockSpec((tile, cols), lambda i: (i, 0))

    low = jax.ShapeDtypeStruct((rows, width), BF16)
    kept = jax.ShapeDtypeStruct((rows, units), BF16)
    return pl.pallas_call(
        expert_last_kernel,
        grid=(rows // tile,),
        in_specs=[tiled(width)] * 3
        + [tiled(1), whole((1, width)), tiled(width), tiled(width), whole(w.shape)],
        out_specs=[tiled(width), tiled(width), whole((1, width)), tiled(units), tiled(units)],
        out_shape=[low, low, jax.ShapeDtypeStruct((1, width), F32), kept, kept],
        scratch_shapes=[pltpu.VMEM((2, units, width), BF16)],
        compiler_params=EXPERT_PARAMS,
        cost_estimate=expert_cost(4, rows, width, hidden, pieces),
        name="expert_last",
    )(x, g, u, gate, cent, out_sum, in_sum, w)


def expert_weights(xt, gt, active, grad_pre, pieces):
    width, rows = xt.shape
    hidden = active.shape[1] // pieces
    kept_spec = pl.BlockSpec((rows, hidden), lambda i: (0, i))
    shape = (pieces, 2, width, hidden)
    return pl.pallas_call(
        expert_weights_kernel,
        grid=(pieces,),
        in_specs=[whole(xt.shape), whole(xt.shape), kept_spec, kept_spec],
        out_specs=pl.BlockSpec((1, *shape[1:]), lambda i: (i, 0, 0, 0)),
        out_shape=jax.ShapeDtypeStruct(shape, BF16),
        compiler_params=EXPERT_PARAMS,
        cost_estimate=expert_cost(2, rows, width, hidden, pieces),
        name="expert_weights",
    )(xt, gt, active, grad_pre)


def norm_back(values, gain, grad):
    centre = jnp.mean(values, -1, keepdims=True)
    centered = values - centre
    spread = jnp.mean(centered * centered, -1, keepdims=True)
    rate = lax.rsqrt(spread + EPSILON)
    standard = centered * rate
    u = grad * gain
    back = rate * (
        u - jnp.mean(u, -1, keepdims=True) - standard * jnp.mean(u * standard, -1, keepdims=True)
    )
    return standard, back


def combine_back_kernel(
    back_ref, target_ref, resid_ref, cot_ref, gain_ref, weight_ref,
    resid_grad_ref, attn_ref, mixed_grad_ref, sums_ref,
):
    @pl.when(pl.program_id(0) == 0)
    def _():
        sums_ref[...] = jnp.zeros_like(sums_ref)

    target = target_ref[...]
    slots = lax.broadcasted_iota(jnp.int32, (1, back_ref.shape[0]), 1)
    grad = dot((target == slots).astype(BF16), back_ref[...])
    standard, back_norm = norm_back(resid_ref[...], gain_ref[...], grad)
    upstream = jnp.where(target >= 0, cot_ref[...].astype(F32), 0.0)
    grad_resid = upstream + back_norm
    resid_grad_ref[...] = grad_resid
    low = grad_resid.astype(BF16)
    attn_ref[...] = low
    mixed_grad_ref[...] = dot_nt(low, weight_ref[...]).astype(BF16)
    sums_ref[0:1, :] += jnp.sum(grad * standard, 0, keepdims=True)
    sums_ref[1:2, :] += jnp.sum(grad, 0, keepdims=True)


def combine_back(back, target, resid, cot, gain, weight):
    length, width = resid.shape
    tile = min(QTILE, length)
    tiled = pl.BlockSpec((tile, width), lambda i: (i, 0))
    low = jax.ShapeDtypeStruct(resid.shape, BF16)
    return pl.pallas_call(
        combine_back_kernel,
        grid=(length // tile,),
        in_specs=[
            whole(back.shape), pl.BlockSpec((tile, 1), lambda i: (i, 0)), tiled, tiled,
            whole((1, width)), whole(weight.shape),
        ],
        out_specs=[tiled, tiled, tiled, whole((8, width))],
        out_shape=[
            jax.ShapeDtypeStruct(resid.shape, F32), low, low, jax.ShapeDtypeStruct((8, width), F32),
        ],
        compiler_params=EXPERT_PARAMS,
        cost_estimate=pl.CostEstimate(
            flops=2 * length * width * (back.shape[0] + width),
            bytes_accessed=20 * length * width,
            transcendentals=0,
        ),
        name="combine_back",
    )(back, target, resid, cot, gain.reshape(1, width), weight)


def combine_out_kernel(rows_ref, target_ref, gate_ref, resid_ref, out_ref):
    slots = lax.broadcasted_iota(jnp.int32, (1, rows_ref.shape[0]), 1)
    rows = dot((target_ref[...] == slots).astype(BF16), rows_ref[...])
    out_ref[0] = (resid_ref[...] + gate_ref[...] * rows).astype(BF16)


def combine_out(rows, target, gate, resid):
    length, width = resid.shape
    tile = min(QTILE, length)
    column = pl.BlockSpec((tile, 1), lambda i: (i, 0))
    return pl.pallas_call(
        combine_out_kernel,
        grid=(length // tile,),
        in_specs=[
            whole(rows.shape), column, column, pl.BlockSpec((tile, width), lambda i: (i, 0)),
        ],
        out_specs=pl.BlockSpec((1, tile, width), lambda i: (0, i, 0)),
        out_shape=jax.ShapeDtypeStruct((1, length, width), BF16),
        compiler_params=EXPERT_PARAMS,
        cost_estimate=pl.CostEstimate(
            flops=2 * length * width * rows.shape[0],
            bytes_accessed=8 * length * width,
            transcendentals=0,
        ),
        name="combine_out",
    )(rows, target, gate, resid)


def finish_experts_kernel(blocks, first_ref, second_ref, hidden_ref, down_ref):
    step = pl.program_id(0)
    for source, here in ((first_ref, step < blocks), (second_ref, step >= blocks)):

        @pl.when(here)
        def _():
            hidden_ref[0] = source[0, 0].astype(F32)
            down_ref[0] = source[0, 1].T.astype(F32)


def finish_experts(first, second):
    unused, two, width, size = second.shape
    blocks = first.shape[3] // size
    hidden = first.shape[3] + size
    return pl.pallas_call(
        functools.partial(finish_experts_kernel, blocks),
        grid=(blocks + 1,),
        in_specs=[
            pl.BlockSpec((1, 2, width, size), lambda i: (0, 0, 0, jnp.minimum(i, blocks - 1))),
            whole(second.shape),
        ],
        out_specs=[
            pl.BlockSpec((1, width, size), lambda i: (0, 0, i)),
            pl.BlockSpec((1, size, width), lambda i: (0, i, 0)),
        ],
        out_shape=[
            jax.ShapeDtypeStruct((1, width, hidden), F32),
            jax.ShapeDtypeStruct((1, hidden, width), F32),
        ],
        compiler_params=EXPERT_PARAMS,
        name="finish_experts",
    )(first, second)


def spread_kernel(
    near, moved, flag_ref, one_ref, one_other, two_ref, two_other,
    query_ref, key_ref, value_ref, output_ref, cent_ref, *vectors,
):
    step = pl.program_id(0)
    steps = pl.num_programs(0)
    half = query_ref.shape[0] // 2
    chains = ((one_ref, one_other), (two_ref, two_other))

    def halves(chain, block):
        cols = pl.ds(pl.multiple_of(block * PAIR, PAIR), PAIR)
        low, high = [side[:, cols].astype(F32) for side in chains[chain]]
        return jnp.where(flag_ref[0] == 0, low, high), jnp.where(flag_ref[0] == 0, high, low)

    for k, here in enumerate((step < near, step >= near)):

        @pl.when(here)
        def _():
            for i, at in enumerate((query_ref, key_ref, value_ref)):
                at[:half, :], at[half:, :] = halves(k, 3 * (step - near * k) + i)

    kept = steps - moved
    sums_at = 3 * (steps - near)
    for k, here in enumerate((step < kept, step >= kept)):

        @pl.when(here)
        def _():
            block = sums_at + 1 + step - kept if k else 3 * near + step
            output_ref[:half, :], output_ref[half:, :] = halves(k, block)

    @pl.when(step == 0)
    def _():
        side = jnp.concatenate([x.T for x in halves(1, sums_at)], 1)
        experts = cent_ref.shape[0]
        cent_ref[...] = side[:experts]
        for ref, row in vectors_of(vectors, experts):
            ref[...] = side[row]


def vectors_of(refs, experts):
    last = experts + 4 + -(experts + 4) % 8
    return zip(refs, range(last - 4, last))


def spread(flag, halves, width, near, moved, experts):
    pairs = width // PAIR
    out = jax.ShapeDtypeStruct((width, width), F32)
    vector = jax.ShapeDtypeStruct((width,), F32)
    return pl.pallas_call(
        functools.partial(spread_kernel, near, moved),
        grid=(pairs,),
        in_specs=[pl.BlockSpec(memory_space=pltpu.SMEM)]
        + [pl.BlockSpec(memory_space=pltpu.VMEM)] * 4,
        out_specs=[pl.BlockSpec((width, PAIR), lambda i: (0, i))] * 4
        + [whole((experts, width))]
        + [whole((width,))] * 4,
        out_shape=[out] * 4 + [jax.ShapeDtypeStruct((experts, width), F32)] + [vector] * 4,
        compiler_params=pltpu.CompilerParams(vmem_limit_bytes=32 * 1024 * 1024),
        name="spread",
    )(flag, *halves[0], *halves[1])


def normalize(values, gain, shift):
    centre = jnp.mean(values, -1, keepdims=True)
    centered = values - centre
    spread = jnp.mean(centered * centered, -1, keepdims=True)
    return centered * lax.rsqrt(spread + EPSILON) * gain + shift


def xor_pairs(size, flip):
    return [(i, i ^ flip) for i in range(size)]


def exchange(rows, blocks):
    shape = rows.shape
    return lax.all_to_all(
        rows.reshape(blocks, -1, shape[1]), "wide", split_axis=0, concat_axis=0, tiled=True
    ).reshape(shape)


def add_up(terms):
    return functools.reduce(lambda a, b: a + b, [t.astype(F32) for t in terms])


def reduce_halves(terms, flags, sizes, bits, beside=None):
    for i, (axis, flip) in enumerate(bits):
        flag = (lax.axis_index(axis) // flip) % 2
        half = terms[0].shape[0] // 2
        mine, theirs = [
            [lax.dynamic_slice_in_dim(t, f * half, half, 0) for t in terms] for f in (flag, 1 - flag)
        ]
        came = lax.ppermute(add_up(theirs).astype(BF16), axis, xor_pairs(sizes[axis], flip))
        if beside is not None and i == len(bits) - 1:
            came, *beside = lax.optimization_barrier((came, *beside))
        terms = [add_up([*mine, came])]
        flags.append(flag)
    return terms[0] if beside is None else (terms[0], *beside)


def gather_halves(total, flags, sizes, bits):
    for at in reversed(range(len(bits))):
        axis, flip = bits[at]
        other = lax.ppermute(total, axis, xor_pairs(sizes[axis], flip))
        total = jnp.where(
            flags[at] == 0, jnp.concatenate([total, other], 0), jnp.concatenate([other, total], 0)
        )
    return total


def gather_plane(one, two, flags, sizes, bits, work, operands):
    columns = two.shape[1]
    for at, (axis, flip) in enumerate(bits):
        back = len(bits) - 1 - at
        came = [
            lax.ppermute(one, bits[back][0], xor_pairs(sizes[bits[back][0]], bits[back][1])),
            lax.ppermute(two, axis, xor_pairs(sizes[axis], flip)),
        ]
        if at == 0:
            came, operands = lax.optimization_barrier((came, operands))
            done = work(*operands)
        if at == len(bits) - 1:
            came, done = lax.optimization_barrier((came, done))
        came_one, came_two = lax.optimization_barrier(came)
        one = jnp.where(
            flags[back] == 0, jnp.concatenate([one, came_one], 0), jnp.concatenate([came_one, one], 0)
        )
        two = jnp.where(
            flags[at] == 0, jnp.stack([two, came_two], at), jnp.stack([came_two, two], at)
        )
    return one, two.reshape(-1, columns), done


def make_shards(n_wide, n_narrow):
    sizes = {"wide": n_wide, "narrow": n_narrow}
    wide_bits = [("wide", 1 << i) for i in range(n_wide.bit_length() - 1)]
    narrow_bits = [("narrow", 1 << i) for i in range(n_narrow.bit_length() - 1)]

    def shards(
        block_in,
        seq_lengths,
        routes,
        first_gain,
        first_shift,
        query_weight,
        key_weight,
        value_weight,
        output_weight,
        second_gain,
        second_shift,
        centroids,
        hidden_weight,
        down_weight,
        cotangent,
    ):
        seqs_here, length, width = block_in.shape
        head_size = width // HEADS
        scale = head_size ** (-0.5)
        tokens = seqs_here * length
        experts_all = centroids.shape[1]
        capacity = 3 * tokens // (2 * experts_all)
        wide_here = lax.axis_index("wide")
        hidden_size = hidden_weight.shape[2]

        second = max(hidden_size // 3 // 128 * 128, 128)
        cuts = (0, hidden_size - second, hidden_size)
        hidden_t = hidden_weight[0].T
        packs = [
            jnp.stack([hidden_t[a:b], down_weight[0, a:b]], 0)[None]
            for a, b in zip(cuts, cuts[1:])
        ]
        packs[0], block_in, seq_lengths, routes, cotangent = lax.optimization_barrier(
            (packs[0], block_in, seq_lengths, routes, cotangent)
        )
        weights = [lax.all_gather(pack, "narrow", axis=0, tiled=True) for pack in packs]

        live = lax.broadcasted_iota(jnp.int32, (tokens,), 0) < seq_lengths[0]
        route = routes.reshape(tokens)
        expert_ids = lax.broadcasted_iota(jnp.int32, (tokens, experts_all), 1)
        picked = route[:, None] == expert_ids
        ones_live = (picked & live[:, None]).astype(jnp.int32)
        earlier = jnp.cumsum(ones_live, 0, dtype=jnp.int32) - ones_live
        slot = jnp.sum(earlier * ones_live, 1, dtype=jnp.int32)
        target = route * capacity + slot
        slot_ids = lax.broadcasted_iota(jnp.int32, (tokens, experts_all * capacity), 1)
        target = jnp.where(live, target, -1)[:, None]
        table = (target == slot_ids).astype(BF16)
        cot = cotangent.reshape(tokens, width)

        def to_slots(rows):
            return dot_tn(table, rows).astype(BF16)

        upstream_slots, block_in, *packs = lax.optimization_barrier(
            (to_slots(cot), block_in, *packs)
        )
        upstream_rows = exchange(upstream_slots, experts_all)

        qkv_weight = jnp.concatenate([query_weight, key_weight, value_weight], 1)
        inputs_wide = block_in.reshape(tokens, width).astype(F32)
        normed_low = normalize(inputs_wide, first_gain, first_shift).astype(BF16)
        projected = dot(normed_low, qkv_weight).astype(BF16)
        mixed, probs = attend(projected, seq_lengths, scale)
        mixed, upstream_rows = lax.optimization_barrier((mixed, upstream_rows))
        resid = inputs_wide + dot(mixed, output_weight)
        normed_second = normalize(resid, second_gain, second_shift).astype(BF16)

        pairs = width // PAIR
        counts = (pairs // 2, pairs // 3, pairs - pairs // 2 - pairs // 3)
        logits = dot(normed_second, centroids)
        gate = jax.nn.sigmoid(jnp.sum(jnp.where(picked, logits, 0.0), 1, keepdims=True))
        slots, normed_t, mixed_t, gate, target = lax.optimization_barrier(
            (to_slots(normed_second), normed_low.T, mixed.T, gate, target)
        )
        rows = exchange(slots, experts_all)
        own_centroid = lax.dynamic_slice_in_dim(centroids.T, wide_here, 1, 0).astype(F32)
        out_sum, in_sum, weight_grads, grad_rows, rows_t, grad_rows_t, row_gate = expert_first(
            rows, upstream_rows, own_centroid, weights[0]
        )
        out_low, back_rows, own_centroid_grad, *kept = expert_last(
            rows, grad_rows, upstream_rows, row_gate, own_centroid, out_sum, in_sum, weights[1]
        )
        back = exchange(back_rows, experts_all)
        more_weight_grads = expert_weights(rows_t, grad_rows_t, *kept, n_narrow)
        own_row = lax.broadcasted_iota(jnp.int32, (experts_all + 4 + -(experts_all + 4) % 8, 1), 0)
        sums = jnp.where(own_row == wide_here, own_centroid_grad, 0.0)
        sums, back = lax.optimization_barrier((sums, back))
        grad_resid, grad_attn, grad_mixed, second_sums = combine_back(
            back, target, resid, cot, second_gain, output_weight
        )
        out_low, more_weight_grads, grad_mixed = lax.optimization_barrier(
            (out_low, more_weight_grads, grad_mixed)
        )
        returned = exchange(out_low, experts_all)

        flag = wide_here % 2
        shared = (flag.reshape(1), projected, grad_mixed, probs, scale)
        core, plane, line = wide_bits[:1], wide_bits[1:], narrow_bits
        flags = [[flag], [flag]]

        def swap(half):
            return lax.ppermute(half, "wide", xor_pairs(n_wide, 1))

        first_summed = lax.psum_scatter(weight_grads, "narrow", scatter_dimension=0, tiled=True)
        mine_one, theirs_one, grads_one = attend_back(
            *shared, counts, 0, normed_t, mixed_t, grad_attn
        )
        came_one = swap(theirs_one)
        mine_two, theirs_two, grads_two = attend_back(*shared, counts, 1, normed_t)
        block_out = combine_out(returned, target, gate, resid)
        grads_two, block_out, came_one, more_weight_grads = lax.optimization_barrier(
            (grads_two, block_out, came_one, more_weight_grads)
        )
        last_summed = lax.psum_scatter(more_weight_grads, "narrow", scatter_dimension=0, tiled=True)
        mine_two, theirs_two, input_grad = attend_back(
            *shared, counts, 2, normed_t, grads_one, grads_two, query_weight, key_weight, value_weight, block_in,
            first_gain.reshape(1, width), grad_resid, sums, second_sums, mine_two, theirs_two,
        )
        chain_one, mine_two, theirs_two, first_summed = reduce_halves(
            [mine_one, came_one], flags[0], sizes, plane[:1], (mine_two, theirs_two, first_summed)
        )
        chain_two = [mine_two, swap(theirs_two)]
        chain_one = reduce_halves([chain_one], flags[0], sizes, plane[1:] + line)
        chain_two = reduce_halves(chain_two, flags[1], sizes, plane[:1])
        chain_two, last_summed = reduce_halves(
            [chain_two], flags[1], sizes, plane[1:] + line, (last_summed,)
        )
        near = [
            gather_halves(total.astype(BF16), kept[len(wide_bits) :], sizes, line)
            for total, kept in zip((chain_one, chain_two), flags)
        ]
        inner = [kept[1 : len(wide_bits)] for kept in flags]
        moved = pairs // 3
        near_cols = near[0].shape[1] - moved * PAIR
        near = [near[0][:, :near_cols], jnp.concatenate([near[1], near[0][:, near_cols:]], 1)]
        *near, (hidden_grad, down_grad) = gather_plane(
            *near, inner[0], sizes, plane, finish_experts, (first_summed, last_summed)
        )
        halves = [(half, swap(half)) for half in near]
        query_grad, key_grad, value_grad, output_weight_grad, centroids_grad, *vectors = spread(
            flag.reshape(1), halves, width, counts[0], moved, experts_all
        )
        centroids_grad = centroids_grad.T
        second_gain_grad, second_shift_grad, first_gain_grad, first_shift_grad = vectors
        return (
            block_out,
            input_grad,
            first_gain_grad,
            first_shift_grad,
            query_grad,
            key_grad,
            value_grad,
            output_weight_grad,
            second_gain_grad,
            second_shift_grad,
            centroids_grad,
            hidden_grad,
            down_grad,
        )

    return shards


def solution(mesh):
    tokens_spec = P(("wide", "narrow"), None, None)
    in_specs = (
        tokens_spec,
        P(("wide", "narrow")),
        tokens_spec,
        *[P()] * 9,
        P("wide", None, "narrow"),
        P("wide", "narrow", None),
        tokens_spec,
    )
    out_specs = (
        tokens_spec,
        tokens_spec,
        *[P()] * 9,
        P("wide", None, "narrow"),
        P("wide", "narrow", None),
    )
    return jax.shard_map(
        make_shards(mesh.shape["wide"], mesh.shape["narrow"]),
        mesh=mesh,
        in_specs=in_specs,
        out_specs=out_specs,
        check_vma=False,
    )
```

```python
import functools
import jax
import jax.numpy as jnp
from jax import lax
from jax.experimental import pallas as pl
from jax.experimental.pallas import tpu as pltpu
from jax.sharding import PartitionSpec as P

F32 = jnp.float32
BF16 = jnp.bfloat16
HEADS = 12
EPSILON = 1e-05
MASKED_SCORE = -1000000000.0
PAIR = 128
QTILE = 256


def dot(left, right):
    return jnp.dot(left, right, preferred_element_type=F32)


def dot_tn(left, right):
    return lax.dot_general(left, right, (((0,), (0,)), ((), ())), preferred_element_type=F32)


def dot_nt(left, right):
    return lax.dot_general(left, right, (((1,), (1,)), ((), ())), preferred_element_type=F32)


def lanes_of(head, shape):
    lane = lax.broadcasted_iota(jnp.int32, shape, 1)
    return (lane >= head * (PAIR // 2)) & (lane < (head + 1) * (PAIR // 2))


def packed_rows(length, tile):
    return [sum(range(1, at + 1)) * tile for at in range(length // tile + 1)]


def attend_kernel(scale, len_ref, q_ref, k_ref, v_ref, mixed_ref, probs_ref):
    length = q_ref.shape[0]
    tile = min(QTILE, length)
    seq_len = len_ref[0]
    starts = packed_rows(length, tile)
    for at in range(length // tile):
        start, finish = at * tile, (at + 1) * tile
        query = q_ref[start:finish, :] * scale
        keys = k_ref[:finish, :]
        values = v_ref[:finish, :]
        key_pos = lax.broadcasted_iota(jnp.int32, (finish, 1), 0)
        bias = jnp.where(key_pos < seq_len, 0.0, MASKED_SCORE)
        row = lax.broadcasted_iota(jnp.int32, (tile, tile), 0)
        col = lax.broadcasted_iota(jnp.int32, (tile, tile), 1)
        mixed = None
        for head in range(2):
            zero = jnp.zeros((), BF16)
            q_head = jnp.where(lanes_of(head, query.shape), query, zero)
            scores = dot_nt(keys, q_head) + bias
            diagonal = jnp.where(row <= col, scores[start:], MASKED_SCORE)
            scores = diagonal if start == 0 else jnp.concatenate([scores[:start], diagonal], 0)
            expo = jnp.exp(scores - jnp.max(scores, 0, keepdims=True))
            probs = (expo * (1.0 / jnp.sum(expo, 0, keepdims=True))).astype(BF16)
            probs_ref[0, head, starts[at] : starts[at + 1], :] = probs
            v_head = jnp.where(lanes_of(head, values.shape), values, zero)
            part = dot_tn(probs, v_head)
            mixed = part if mixed is None else mixed + part
        mixed_ref[start:finish, :] = mixed.astype(BF16)


def attend(projected, seq_lengths, scale):
    length, width3 = projected.shape
    width = width3 // 3
    pairs = width // PAIR
    tile = min(QTILE, length)
    rows = packed_rows(length, tile)[-1]
    return pl.pallas_call(
        functools.partial(attend_kernel, scale),
        grid_spec=pltpu.PrefetchScalarGridSpec(
            num_scalar_prefetch=1,
            grid=(pairs,),
            in_specs=[
                pl.BlockSpec((length, PAIR), lambda i, s: (0, i)),
                pl.BlockSpec((length, PAIR), lambda i, s: (0, pairs + i)),
                pl.BlockSpec((length, PAIR), lambda i, s: (0, 2 * pairs + i)),
            ],
            out_specs=[
                pl.BlockSpec((length, PAIR), lambda i, s: (0, i)),
                pl.BlockSpec((1, 2, rows, tile), lambda i, s: (i, 0, 0, 0)),
            ],
        ),
        out_shape=[
            jax.ShapeDtypeStruct((length, width), BF16),
            jax.ShapeDtypeStruct((pairs, 2, rows, tile), BF16),
        ],
        compiler_params=pltpu.CompilerParams(vmem_limit_bytes=48 * 1024 * 1024),
        cost_estimate=pl.CostEstimate(
            flops=4 * length * length * width, bytes_accessed=8 * length * width, transcendentals=0
        ),
        name="attend",
    )(seq_lengths, projected, projected, projected)


def attend_back_kernel(
    scale, counts, part, flag_ref, q_ref, k_ref, v_ref, g_ref, probs_ref, normed_t, *refs
):
    parts = len(counts)
    count = counts[part]
    last = part == parts - 1
    if part == 0:
        mixed_t, attn_ref, mine_ref, theirs_ref, grads = refs
    elif last:
        befores, refs = refs[: parts - 1], refs[parts - 1 :]
        qkv, (in_ref, gain_ref, resid_ref, cent_ref, sums_ref) = refs[:3], refs[3:8]
        mine_ref, theirs_ref, out_ref, grads, sums_scratch = refs[10:]
    else:
        mine_ref, theirs_ref, grads = refs
    length = q_ref.shape[0]
    tile = min(QTILE, length)
    starts = packed_rows(length, tile)
    step = pl.program_id(0)
    half = mine_ref.shape[0]
    columns = 3 * PAIR

    def give(product):
        low, high = product[:half], product[half:]
        mine_ref[...] = jnp.where(flag_ref[0] == 0, low, high)
        theirs_ref[...] = jnp.where(flag_ref[0] == 0, high, low).astype(BF16)

    def pair():
        dk_sum = [None] * (length // tile)
        dv_sum = [None] * (length // tile)
        dq = []
        for at in range(length // tile):
            start, finish = at * tile, (at + 1) * tile
            query = q_ref[start:finish, :] * scale
            grad = g_ref[start:finish, :]
            keys = k_ref[:finish, :]
            values = v_ref[:finish, :]
            grad_query = None
            for head in range(2):
                zero = jnp.zeros((), BF16)
                q_head = jnp.where(lanes_of(head, query.shape), query, zero)
                g_head = jnp.where(lanes_of(head, query.shape), grad, zero)
                k_head = jnp.where(lanes_of(head, keys.shape), keys, zero)
                low = probs_ref[0, head, starts[at] : starts[at + 1], :]
                probs = low.astype(F32)
                product = probs * dot_nt(values, g_head)
                centre = jnp.sum(product, 0, keepdims=True)
                grad_scores = (product - probs * centre).astype(BF16)
                dv = dot(low, g_head)
                dk = dot(grad_scores, q_head)
                for j in range(at + 1):
                    here = slice(j * tile, (j + 1) * tile)
                    dk_sum[j] = dk[here] if dk_sum[j] is None else dk_sum[j] + dk[here]
                    dv_sum[j] = dv[here] if dv_sum[j] is None else dv_sum[j] + dv[here]
                share = dot_tn(grad_scores, k_head)
                grad_query = share if grad_query is None else grad_query + share
            dq.append((grad_query * scale).astype(BF16))
        sides = [dq, [x.astype(BF16) for x in dk_sum], [x.astype(BF16) for x in dv_sum]]
        return jnp.concatenate([jnp.concatenate(side, 0) for side in sides], 1)

    @pl.when(step < count)
    def _():
        found = pair()
        for k in range(3):
            cols = pl.ds(pl.multiple_of(step * PAIR, PAIR), PAIR) if last else slice(None)
            grads[k, :, cols] = found[:, k * PAIR : (k + 1) * PAIR]
        give(dot(normed_t[...], found))

    if part == 0:

        @pl.when(step >= count)
        def _():
            give(dot(mixed_t[...], attn_ref[...]))

    if last:

        @pl.when(step == count)
        def _():
            sums_scratch[...] = jnp.zeros_like(sums_scratch)

        @pl.when(step >= count)
        def _():
            here = pl.ds(pl.multiple_of((step - count) * tile, tile), tile)
            grad = None
            for j in range(parts):
                before = sum(counts[:j])
                cols = slice(before * PAIR, (before + counts[j]) * PAIR)
                for k, weight in enumerate(qkv):
                    side = grads[k, here, :] if j == parts - 1 else befores[j][k]
                    share = dot_nt(side, weight[:, cols])
                    grad = share if grad is None else grad + share
            standard, back_norm = norm_back(in_ref[0].astype(F32), gain_ref[...], grad)
            out_ref[0] = (resid_ref[...] + back_norm).astype(BF16)
            sums_scratch[0:1, :] += jnp.sum(grad * standard, 0, keepdims=True)
            sums_scratch[1:2, :] += jnp.sum(grad, 0, keepdims=True)

        @pl.when(step == count + length // tile - 1)
        def _():
            sums = cent_ref[...]
            rows, width = sums.shape
            place = lax.broadcasted_iota(jnp.int32, (rows, 1), 0)
            for row, ref, k in (
                (rows - 4, sums_ref, 0), (rows - 3, sums_ref, 1),
                (rows - 2, sums_scratch, 0), (rows - 1, sums_scratch, 1),
            ):
                sums = jnp.where(place == row, ref[k : k + 1, :], sums)
            turned = jnp.concatenate([sums, jnp.zeros((PAIR - rows, width), F32)], 0).T
            low, high = turned[:half], turned[half:]
            mine_ref[:, :PAIR] = jnp.where(flag_ref[0] == 0, low, high)
            theirs_ref[:, :PAIR] = jnp.where(flag_ref[0] == 0, high, low).astype(BF16)


def attend_back(flag, projected, grad_mixed, probs, scale, counts, part, normed_t, *more):
    width, length = normed_t.shape
    pairs = width // PAIR
    count = counts[part]
    first = sum(counts[:part])
    last = part == len(counts) - 1
    block = (length, PAIR)
    columns = 3 * PAIR
    extra = width // columns if part == 0 else 0

    def at(i):
        return first + jnp.minimum(i, count - 1)

    own = (count + extra) * columns
    held = own if part == 0 else sum(counts[1:]) * columns + PAIR
    offset = sum(counts[1:part])
    steps = count + (1 if last else extra)
    half_spec = pl.BlockSpec(
        (width // 2, columns), lambda i, s: (0, offset + jnp.minimum(i, steps - 1))
    )
    half_shape = (width // 2, held)
    in_specs = [
        pl.BlockSpec(block, lambda i, s: (0, at(i))),
        pl.BlockSpec(block, lambda i, s: (0, pairs + at(i))),
        pl.BlockSpec(block, lambda i, s: (0, 2 * pairs + at(i))),
        pl.BlockSpec(block, lambda i, s: (0, at(i))),
        pl.BlockSpec((1, *probs.shape[1:]), lambda i, s: (at(i), 0, 0, 0)),
        whole(normed_t.shape),
    ]
    out_specs = [half_spec, half_spec]
    out_shape = [jax.ShapeDtypeStruct(half_shape, F32), jax.ShapeDtypeStruct(half_shape, BF16)]
    scratch = []
    aliases = {}
    if last:
        tile = min(QTILE, length)

        def row(i):
            return jnp.maximum(i - count, 0)

        in_specs += [
            pl.BlockSpec((3, tile, c * PAIR), lambda i, s: (0, row(i), 0)) for c in counts[:-1]
        ]
        in_specs += [whole((width, width))] * 3
        in_specs += [
            pl.BlockSpec((1, tile, width), lambda i, s: (0, row(i), 0)), whole((1, width)),
            pl.BlockSpec((tile, width), lambda i, s: (row(i), 0)), whole(more[-4].shape),
            whole(more[-3].shape),
        ]
        in_specs += [pl.BlockSpec(memory_space=pl.ANY)] * 2
        aliases = {5 + len(more): 0, 6 + len(more): 1}
        extra = length // tile
        out_specs += [pl.BlockSpec((1, tile, width), lambda i, s: (0, row(i), 0))]
        out_shape += [jax.ShapeDtypeStruct((1, length, width), BF16)]
        scratch += [pltpu.VMEM((3, length, count * PAIR), BF16), pltpu.VMEM((8, width), F32)]
    else:
        if part == 0:
            in_specs += [
                whole((width, length)),
                pl.BlockSpec((length, columns), lambda i, s: (0, jnp.maximum(i - count, 0))),
            ]
        out_specs += [
            pl.BlockSpec((3, length, PAIR), lambda i, s: (0, 0, jnp.minimum(i, count - 1)))
        ]
        out_shape += [jax.ShapeDtypeStruct((3, length, count * PAIR), BF16)]
    return pl.pallas_call(
        functools.partial(attend_back_kernel, scale, counts, part),
        grid_spec=pltpu.PrefetchScalarGridSpec(
            num_scalar_prefetch=1,
            grid=(count + extra,),
            in_specs=in_specs,
            out_specs=out_specs,
            scratch_shapes=scratch,
        ),
        out_shape=out_shape,
        input_output_aliases=aliases,
        compiler_params=pltpu.CompilerParams(vmem_limit_bytes=58 * 1024 * 1024),
        cost_estimate=pl.CostEstimate(
            flops=20 * length * length * count * PAIR,
            bytes_accessed=14 * length * count * PAIR,
            transcendentals=0,
        ),
        name="attend_back",
    )(flag, projected, projected, projected, grad_mixed, probs, normed_t, *more)


ERFC = (0.254829592, -0.284496736, 1.421413741, -1.453152027, 1.061405429)
ERFC_RATE = 0.3275911 * 0.5**0.5
ROWS = 256


def gelu_pair(value):
    size = jnp.abs(value)
    t = 1.0 / (1.0 + ERFC_RATE * size)
    poly = t * (
        ERFC[0] + t * (ERFC[1] + t * (ERFC[2] + t * (ERFC[3] + t * ERFC[4])))
    )
    bell = jnp.exp(-0.5 * value * value)
    tail = 0.5 * poly * bell
    below = jnp.where(value < 0, tail, 1.0 - tail)
    return value * below, below + value * (bell * 0.3989422804014327)


def join_pieces(w_ref, w_all):
    pieces, unused, hidden, unused_width = w_ref.shape
    for p in range(pieces):
        for k in range(2):
            w_all[k, p * hidden : (p + 1) * hidden, :] = w_ref[p, k]


def expert_tile(x, g, w_all, active_ref, pre_ref, at):
    units = w_all.shape[1]
    chunk = units if units <= 512 else 512 if units % 512 == 0 else 384
    for start in range(0, units, chunk):
        cols = slice(start, start + chunk)
        active, slope = gelu_pair(dot_nt(x, w_all[0, cols, :]))
        active_ref[at, cols] = active.astype(BF16)
        pre_ref[at, cols] = (dot_nt(g, w_all[1, cols, :]) * slope).astype(BF16)
    return dot(active_ref[at, :], w_all[1]), dot(pre_ref[at, :], w_all[0])


def expert_first_kernel(
    tiles, x_ref, u_ref, cent_ref, w_ref, out_ref, in_ref, dw_ref, g_ref, xt_ref, gt_ref, gate_ref,
    active, grad_pre, w_all,
):
    rows = x_ref.shape[0]
    step = pl.program_id(0)

    @pl.when(step == 0)
    def _():
        join_pieces(w_ref, w_all)

    @pl.when(step < tiles)
    def _():
        at = pl.ds(pl.multiple_of(step * rows, rows), rows)
        x = x_ref[...]
        chosen = jnp.sum(x.astype(F32) * cent_ref[...], 1, keepdims=True)
        gate = 1.0 / (1.0 + jnp.exp(-chosen))
        gate_ref[...] = gate
        g = (gate * u_ref[...].astype(F32)).astype(BF16)
        g_ref[...] = g
        xt_ref[:, at] = x.T
        gt_ref[:, at] = g.T
        out_ref[...], in_ref[...] = expert_tile(x, g, w_all, active, grad_pre, at)

    @pl.when(step >= tiles)
    def _():
        hidden = dw_ref.shape[3]
        cols = pl.ds(pl.multiple_of((step - tiles) * hidden, hidden), hidden)
        dw_ref[0, 0] = dot(xt_ref[...], grad_pre[:, cols]).astype(BF16)
        dw_ref[0, 1] = dot(gt_ref[...], active[:, cols]).astype(BF16)


def expert_last_kernel(
    x_ref, g_ref, u_ref, gate_ref, cent_ref, out_in, in_in, w_ref,
    low_ref, back_ref, cent_grad_ref, active_ref, pre_ref, w_all,
):
    @pl.when(pl.program_id(0) == 0)
    def _():
        join_pieces(w_ref, w_all)
        cent_grad_ref[...] = jnp.zeros_like(cent_grad_ref)

    x = x_ref[...]
    out, grad_in = expert_tile(x, g_ref[...], w_all, active_ref, pre_ref, slice(None))
    low = (out_in[...] + out).astype(BF16)
    low_ref[...] = low
    gate = gate_ref[...]
    chosen = jnp.sum(u_ref[...].astype(F32) * low.astype(F32), 1, keepdims=True)
    chosen = chosen * gate * (1.0 - gate)
    back_ref[...] = (in_in[...] + grad_in + chosen * cent_ref[...]).astype(BF16)
    cent_grad_ref[...] += jnp.sum(chosen * x.astype(F32), 0, keepdims=True)


def expert_weights_kernel(xt_ref, gt_ref, active_ref, pre_ref, hidden_ref, down_ref):
    hidden_ref[0] = dot(xt_ref[...], pre_ref[...]).astype(BF16)
    down_ref[0] = dot(gt_ref[...], active_ref[...]).astype(BF16)


def whole(shape):
    return pl.BlockSpec(shape, lambda *i: (0,) * len(shape), pipeline_mode=pl.Buffered(1))


EXPERT_PARAMS = pltpu.CompilerParams(vmem_limit_bytes=58 * 1024 * 1024)


def expert_cost(kind, rows, width, hidden, pieces):
    return pl.CostEstimate(
        flops=2 * kind * rows * width * hidden * pieces,
        bytes_accessed=6 * rows * width * 4,
        transcendentals=0,
    )


def expert_first(x, u, cent, w):
    rows, width = x.shape
    pieces, unused, hidden, unused_width = w.shape
    tile = min(ROWS, rows)
    tiles = rows // tile
    units = pieces * hidden

    def tiled(cols):
        return pl.BlockSpec((tile, cols), lambda i: (jnp.minimum(i, tiles - 1), 0))

    wide = jax.ShapeDtypeStruct((rows, width), F32)
    turned = jax.ShapeDtypeStruct((width, rows), BF16)
    return pl.pallas_call(
        functools.partial(expert_first_kernel, tiles),
        grid=(tiles + pieces,),
        in_specs=[tiled(width), tiled(width), whole((1, width)), whole(w.shape)],
        out_specs=[
            tiled(width), tiled(width),
            pl.BlockSpec((1, 2, width, hidden), lambda i: (jnp.maximum(i - tiles, 0), 0, 0, 0)),
            tiled(width), whole(turned.shape), whole(turned.shape), tiled(1),
        ],
        out_shape=[
            wide, wide, jax.ShapeDtypeStruct((pieces, 2, width, hidden), BF16),
            jax.ShapeDtypeStruct((rows, width), BF16), turned, turned,
            jax.ShapeDtypeStruct((rows, 1), F32),
        ],
        scratch_shapes=[
            pltpu.VMEM((rows, units), BF16), pltpu.VMEM((rows, units), BF16),
            pltpu.VMEM((2, units, width), BF16),
        ],
        compiler_params=EXPERT_PARAMS,
        cost_estimate=expert_cost(6, rows, width, hidden, pieces),
        name="expert_first",
    )(x, u, cent, w)


def expert_last(x, g, u, gate, cent, out_sum, in_sum, w):
    rows, width = x.shape
    pieces, unused, hidden, unused_width = w.shape
    tile = min(ROWS, rows)
    units = pieces * hidden

    def tiled(cols):
        return pl.BlockSpec((tile, cols), lambda i: (i, 0))

    low = jax.ShapeDtypeStruct((rows, width), BF16)
    kept = jax.ShapeDtypeStruct((rows, units), BF16)
    return pl.pallas_call(
        expert_last_kernel,
        grid=(rows // tile,),
        in_specs=[tiled(width)] * 3
        + [tiled(1), whole((1, width)), tiled(width), tiled(width), whole(w.shape)],
        out_specs=[tiled(width), tiled(width), whole((1, width)), tiled(units), tiled(units)],
        out_shape=[low, low, jax.ShapeDtypeStruct((1, width), F32), kept, kept],
        scratch_shapes=[pltpu.VMEM((2, units, width), BF16)],
        compiler_params=EXPERT_PARAMS,
        cost_estimate=expert_cost(4, rows, width, hidden, pieces),
        name="expert_last",
    )(x, g, u, gate, cent, out_sum, in_sum, w)


def expert_weights(xt, gt, active, grad_pre, pieces):
    width, rows = xt.shape
    hidden = active.shape[1] // pieces
    kept_spec = pl.BlockSpec((rows, hidden), lambda i: (0, i))
    shape = (pieces, width, hidden)
    piece = pl.BlockSpec((1, width, hidden), lambda i: (i, 0, 0))
    return pl.pallas_call(
        expert_weights_kernel,
        grid=(pieces,),
        in_specs=[whole(xt.shape), whole(xt.shape), kept_spec, kept_spec],
        out_specs=[piece, piece],
        out_shape=[jax.ShapeDtypeStruct(shape, BF16)] * 2,
        compiler_params=EXPERT_PARAMS,
        cost_estimate=expert_cost(2, rows, width, hidden, pieces),
        name="expert_weights",
    )(xt, gt, active, grad_pre)


def norm_back(values, gain, grad):
    centre = jnp.mean(values, -1, keepdims=True)
    centered = values - centre
    spread = jnp.mean(centered * centered, -1, keepdims=True)
    rate = lax.rsqrt(spread + EPSILON)
    standard = centered * rate
    u = grad * gain
    back = rate * (
        u - jnp.mean(u, -1, keepdims=True) - standard * jnp.mean(u * standard, -1, keepdims=True)
    )
    return standard, back


def combine_back_kernel(
    back_ref, target_ref, resid_ref, cot_ref, gain_ref, weight_ref,
    resid_grad_ref, attn_ref, mixed_grad_ref, sums_ref,
):
    @pl.when(pl.program_id(0) == 0)
    def _():
        sums_ref[...] = jnp.zeros_like(sums_ref)

    target = target_ref[...]
    slots = lax.broadcasted_iota(jnp.int32, (1, back_ref.shape[0]), 1)
    grad = dot((target == slots).astype(BF16), back_ref[...])
    standard, back_norm = norm_back(resid_ref[...], gain_ref[...], grad)
    upstream = jnp.where(target >= 0, cot_ref[...].astype(F32), 0.0)
    grad_resid = upstream + back_norm
    resid_grad_ref[...] = grad_resid
    low = grad_resid.astype(BF16)
    attn_ref[...] = low
    mixed_grad_ref[...] = dot_nt(low, weight_ref[...]).astype(BF16)
    sums_ref[0:1, :] += jnp.sum(grad * standard, 0, keepdims=True)
    sums_ref[1:2, :] += jnp.sum(grad, 0, keepdims=True)


def combine_back(back, target, resid, cot, gain, weight):
    length, width = resid.shape
    tile = min(QTILE, length)
    tiled = pl.BlockSpec((tile, width), lambda i: (i, 0))
    low = jax.ShapeDtypeStruct(resid.shape, BF16)
    return pl.pallas_call(
        combine_back_kernel,
        grid=(length // tile,),
        in_specs=[
            whole(back.shape), pl.BlockSpec((tile, 1), lambda i: (i, 0)), tiled, tiled,
            whole((1, width)), whole(weight.shape),
        ],
        out_specs=[tiled, tiled, tiled, whole((8, width))],
        out_shape=[
            jax.ShapeDtypeStruct(resid.shape, F32), low, low, jax.ShapeDtypeStruct((8, width), F32),
        ],
        compiler_params=EXPERT_PARAMS,
        cost_estimate=pl.CostEstimate(
            flops=2 * length * width * (back.shape[0] + width),
            bytes_accessed=20 * length * width,
            transcendentals=0,
        ),
        name="combine_back",
    )(back, target, resid, cot, gain.reshape(1, width), weight)


def combine_out_kernel(rows_ref, target_ref, gate_ref, resid_ref, out_ref):
    slots = lax.broadcasted_iota(jnp.int32, (1, rows_ref.shape[0]), 1)
    rows = dot((target_ref[...] == slots).astype(BF16), rows_ref[...])
    out_ref[0] = (resid_ref[...] + gate_ref[...] * rows).astype(BF16)


def combine_out(rows, target, gate, resid):
    length, width = resid.shape
    tile = min(QTILE, length)
    column = pl.BlockSpec((tile, 1), lambda i: (i, 0))
    return pl.pallas_call(
        combine_out_kernel,
        grid=(length // tile,),
        in_specs=[
            whole(rows.shape), column, column, pl.BlockSpec((tile, width), lambda i: (i, 0)),
        ],
        out_specs=pl.BlockSpec((1, tile, width), lambda i: (0, i, 0)),
        out_shape=jax.ShapeDtypeStruct((1, length, width), BF16),
        compiler_params=EXPERT_PARAMS,
        cost_estimate=pl.CostEstimate(
            flops=2 * length * width * rows.shape[0],
            bytes_accessed=8 * length * width,
            transcendentals=0,
        ),
        name="combine_out",
    )(rows, target, gate, resid)


def finish_experts_kernel(blocks, turned, first_ref, second_ref, out_ref):
    step = pl.program_id(0)

    def put(rows):
        out_ref[0] = (rows.T if turned else rows).astype(F32)

    @pl.when(step < blocks)
    def _():
        put(first_ref[0, 0])

    @pl.when(step >= blocks)
    def _():
        put(second_ref[0])


def finish_experts(first, second, index):
    unused, width, size = second.shape
    blocks = first.shape[3] // size
    hidden = first.shape[3] + size
    turned = index == 1
    block, shape = (1, width, size), (1, width, hidden)
    if turned:
        block, shape = (1, size, width), (1, hidden, width)
    return pl.pallas_call(
        functools.partial(finish_experts_kernel, blocks, turned),
        grid=(blocks + 1,),
        in_specs=[
            pl.BlockSpec((1, 1, width, size), lambda i: (0, index, 0, jnp.minimum(i, blocks - 1))),
            whole(second.shape),
        ],
        out_specs=pl.BlockSpec(block, lambda i: (0, i, 0) if turned else (0, 0, i)),
        out_shape=jax.ShapeDtypeStruct(shape, F32),
        compiler_params=EXPERT_PARAMS,
        name="finish_experts",
    )(first, second)


def spread_kernel(
    near, moved, flag_ref, one_ref, one_other, two_ref, two_other,
    query_ref, key_ref, value_ref, output_ref, cent_ref, *vectors,
):
    step = pl.program_id(0)
    steps = pl.num_programs(0)
    half = query_ref.shape[0] // 2
    chains = ((one_ref, one_other), (two_ref, two_other))

    def halves(chain, block):
        cols = pl.ds(pl.multiple_of(block * PAIR, PAIR), PAIR)
        low, high = [side[:, cols].astype(F32) for side in chains[chain]]
        return jnp.where(flag_ref[0] == 0, low, high), jnp.where(flag_ref[0] == 0, high, low)

    for k, here in enumerate((step < near, step >= near)):

        @pl.when(here)
        def _():
            for i, at in enumerate((query_ref, key_ref, value_ref)):
                at[:half, :], at[half:, :] = halves(k, 3 * (step - near * k) + i)

    kept = steps - moved
    sums_at = 3 * (steps - near)
    for k, here in enumerate((step < kept, step >= kept)):

        @pl.when(here)
        def _():
            block = sums_at + 1 + step - kept if k else 3 * near + step
            output_ref[:half, :], output_ref[half:, :] = halves(k, block)

    @pl.when(step == 0)
    def _():
        side = jnp.concatenate([x.T for x in halves(1, sums_at)], 1)
        experts = cent_ref.shape[0]
        cent_ref[...] = side[:experts]
        for ref, row in vectors_of(vectors, experts):
            ref[...] = side[row]


def vectors_of(refs, experts):
    last = experts + 4 + -(experts + 4) % 8
    return zip(refs, range(last - 4, last))


def spread(flag, halves, width, near, moved, experts):
    pairs = width // PAIR
    out = jax.ShapeDtypeStruct((width, width), F32)
    vector = jax.ShapeDtypeStruct((width,), F32)
    return pl.pallas_call(
        functools.partial(spread_kernel, near, moved),
        grid=(pairs,),
        in_specs=[pl.BlockSpec(memory_space=pltpu.SMEM)]
        + [pl.BlockSpec(memory_space=pltpu.VMEM)] * 4,
        out_specs=[pl.BlockSpec((width, PAIR), lambda i: (0, i))] * 4
        + [whole((experts, width))]
        + [whole((width,))] * 4,
        out_shape=[out] * 4 + [jax.ShapeDtypeStruct((experts, width), F32)] + [vector] * 4,
        compiler_params=pltpu.CompilerParams(vmem_limit_bytes=32 * 1024 * 1024),
        name="spread",
    )(flag, *halves[0], *halves[1])


def normalize(values, gain, shift):
    centre = jnp.mean(values, -1, keepdims=True)
    centered = values - centre
    spread = jnp.mean(centered * centered, -1, keepdims=True)
    return centered * lax.rsqrt(spread + EPSILON) * gain + shift


def xor_pairs(size, flip):
    return [(i, i ^ flip) for i in range(size)]


def exchange(rows, blocks):
    shape = rows.shape
    return lax.all_to_all(
        rows.reshape(blocks, -1, shape[1]), "wide", split_axis=0, concat_axis=0, tiled=True
    ).reshape(shape)


def add_up(terms):
    return functools.reduce(lambda a, b: a + b, [t.astype(F32) for t in terms])


def reduce_halves(terms, flags, sizes, bits, beside=None):
    for i, (axis, flip) in enumerate(bits):
        flag = (lax.axis_index(axis) // flip) % 2
        half = terms[0].shape[0] // 2
        mine, theirs = [
            [lax.dynamic_slice_in_dim(t, f * half, half, 0) for t in terms] for f in (flag, 1 - flag)
        ]
        came = lax.ppermute(add_up(theirs).astype(BF16), axis, xor_pairs(sizes[axis], flip))
        if beside is not None and i == len(bits) - 1:
            came, *beside = lax.optimization_barrier((came, *beside))
        terms = [add_up([*mine, came])]
        flags.append(flag)
    return terms[0] if beside is None else (terms[0], *beside)


def gather_halves(total, flags, sizes, bits):
    for at in reversed(range(len(bits))):
        axis, flip = bits[at]
        other = lax.ppermute(total, axis, xor_pairs(sizes[axis], flip))
        total = jnp.where(
            flags[at] == 0, jnp.concatenate([total, other], 0), jnp.concatenate([other, total], 0)
        )
    return total


def gather_plane(one, two, flags, sizes, bits, work, operands):
    columns = two.shape[1]
    for at, (axis, flip) in enumerate(bits):
        back = len(bits) - 1 - at
        came = [
            lax.ppermute(one, bits[back][0], xor_pairs(sizes[bits[back][0]], bits[back][1])),
            lax.ppermute(two, axis, xor_pairs(sizes[axis], flip)),
        ]
        if at == 0:
            came, operands = lax.optimization_barrier((came, operands))
            done = work(*operands)
        if at == len(bits) - 1:
            came, done = lax.optimization_barrier((came, done))
        came_one, came_two = lax.optimization_barrier(came)
        one = jnp.where(
            flags[back] == 0, jnp.concatenate([one, came_one], 0), jnp.concatenate([came_one, one], 0)
        )
        two = jnp.where(
            flags[at] == 0, jnp.stack([two, came_two], at), jnp.stack([came_two, two], at)
        )
    return one, two.reshape(-1, columns), done


def make_shards(n_wide, n_narrow):
    sizes = {"wide": n_wide, "narrow": n_narrow}
    wide_bits = [("wide", 1 << i) for i in range(n_wide.bit_length() - 1)]
    narrow_bits = [("narrow", 1 << i) for i in range(n_narrow.bit_length() - 1)]

    def shards(
        block_in,
        seq_lengths,
        routes,
        first_gain,
        first_shift,
        query_weight,
        key_weight,
        value_weight,
        output_weight,
        second_gain,
        second_shift,
        centroids,
        hidden_weight,
        down_weight,
        cotangent,
    ):
        seqs_here, length, width = block_in.shape
        head_size = width // HEADS
        scale = head_size ** (-0.5)
        tokens = seqs_here * length
        experts_all = centroids.shape[1]
        capacity = 3 * tokens // (2 * experts_all)
        wide_here = lax.axis_index("wide")
        hidden_size = hidden_weight.shape[2]

        second = max(hidden_size // 3 // 128 * 128, 128)
        cuts = (0, hidden_size - second, hidden_size)
        hidden_t = hidden_weight[0].T
        packs = [
            jnp.stack([hidden_t[a:b], down_weight[0, a:b]], 0)[None]
            for a, b in zip(cuts, cuts[1:])
        ]
        packs[0], block_in, seq_lengths, routes, cotangent = lax.optimization_barrier(
            (packs[0], block_in, seq_lengths, routes, cotangent)
        )
        weights = [lax.all_gather(pack, "narrow", axis=0, tiled=True) for pack in packs]

        live = lax.broadcasted_iota(jnp.int32, (tokens,), 0) < seq_lengths[0]
        route = routes.reshape(tokens)
        expert_ids = lax.broadcasted_iota(jnp.int32, (tokens, experts_all), 1)
        picked = route[:, None] == expert_ids
        ones_live = (picked & live[:, None]).astype(jnp.int32)
        earlier = jnp.cumsum(ones_live, 0, dtype=jnp.int32) - ones_live
        slot = jnp.sum(earlier * ones_live, 1, dtype=jnp.int32)
        target = route * capacity + slot
        slot_ids = lax.broadcasted_iota(jnp.int32, (tokens, experts_all * capacity), 1)
        target = jnp.where(live, target, -1)[:, None]
        table = (target == slot_ids).astype(BF16)
        cot = cotangent.reshape(tokens, width)

        def to_slots(rows):
            return dot_tn(table, rows).astype(BF16)

        upstream_slots, block_in, *packs = lax.optimization_barrier(
            (to_slots(cot), block_in, *packs)
        )
        upstream_rows = exchange(upstream_slots, experts_all)

        qkv_weight = jnp.concatenate([query_weight, key_weight, value_weight], 1)
        inputs_wide = block_in.reshape(tokens, width).astype(F32)
        normed_low = normalize(inputs_wide, first_gain, first_shift).astype(BF16)
        projected = dot(normed_low, qkv_weight).astype(BF16)
        mixed, probs = attend(projected, seq_lengths, scale)
        mixed, upstream_rows = lax.optimization_barrier((mixed, upstream_rows))
        resid = inputs_wide + dot(mixed, output_weight)
        normed_second = normalize(resid, second_gain, second_shift).astype(BF16)

        pairs = width // PAIR
        counts = (pairs // 2, pairs // 3, pairs - pairs // 2 - pairs // 3)
        logits = dot(normed_second, centroids)
        gate = jax.nn.sigmoid(jnp.sum(jnp.where(picked, logits, 0.0), 1, keepdims=True))
        slots, normed_t, mixed_t, gate, target = lax.optimization_barrier(
            (to_slots(normed_second), normed_low.T, mixed.T, gate, target)
        )
        rows = exchange(slots, experts_all)
        own_centroid = lax.dynamic_slice_in_dim(centroids.T, wide_here, 1, 0).astype(F32)
        out_sum, in_sum, weight_grads, grad_rows, rows_t, grad_rows_t, row_gate = expert_first(
            rows, upstream_rows, own_centroid, weights[0]
        )
        out_low, back_rows, own_centroid_grad, *kept = expert_last(
            rows, grad_rows, upstream_rows, row_gate, own_centroid, out_sum, in_sum, weights[1]
        )
        back = exchange(back_rows, experts_all)
        more_hidden, more_down = expert_weights(rows_t, grad_rows_t, *kept, n_narrow)
        own_row = lax.broadcasted_iota(jnp.int32, (experts_all + 4 + -(experts_all + 4) % 8, 1), 0)
        sums = jnp.where(own_row == wide_here, own_centroid_grad, 0.0)
        sums, back = lax.optimization_barrier((sums, back))
        grad_resid, grad_attn, grad_mixed, second_sums = combine_back(
            back, target, resid, cot, second_gain, output_weight
        )
        out_low, more_hidden, more_down, grad_mixed = lax.optimization_barrier(
            (out_low, more_hidden, more_down, grad_mixed)
        )
        returned = exchange(out_low, experts_all)

        flag = wide_here % 2
        shared = (flag.reshape(1), projected, grad_mixed, probs, scale)
        core, plane, line = wide_bits[:1], wide_bits[1:], narrow_bits
        flags = [[flag], [flag]]

        def swap(half):
            return lax.ppermute(half, "wide", xor_pairs(n_wide, 1))

        first_summed = lax.psum_scatter(weight_grads, "narrow", scatter_dimension=0, tiled=True)
        mine_one, theirs_one, grads_one = attend_back(
            *shared, counts, 0, normed_t, mixed_t, grad_attn
        )
        came_one = swap(theirs_one)
        mine_two, theirs_two, grads_two = attend_back(*shared, counts, 1, normed_t)
        grads_two, returned, came_one, more_hidden = lax.optimization_barrier(
            (grads_two, returned, came_one, more_hidden)
        )
        hidden_summed = lax.psum_scatter(more_hidden, "narrow", scatter_dimension=0, tiled=True)
        mine_two, theirs_two, input_grad = attend_back(
            *shared, counts, 2, normed_t, grads_one, grads_two, query_weight, key_weight, value_weight, block_in,
            first_gain.reshape(1, width), grad_resid, sums, second_sums, mine_two, theirs_two,
        )
        chain_one, mine_two, theirs_two, first_summed = reduce_halves(
            [mine_one, came_one], flags[0], sizes, plane[:1], (mine_two, theirs_two, first_summed)
        )
        chain_two = [mine_two, swap(theirs_two)]
        chain_one = reduce_halves([chain_one], flags[0], sizes, plane[1:] + line)
        chain_two = reduce_halves(chain_two, flags[1], sizes, plane[:1])
        chain_two, hidden_summed = reduce_halves(
            [chain_two], flags[1], sizes, plane[1:], (hidden_summed,)
        )
        chain_two = reduce_halves([chain_two], flags[1], sizes, line)
        near = [
            gather_halves(total.astype(BF16), kept[-len(line) :], sizes, line)
            for total, kept in ((chain_one, flags[0]),)
        ]
        kept = flags[1][-len(line) :]
        far = gather_halves(chain_two.astype(BF16), kept[1:], sizes, line[1:])
        far, more_down = lax.optimization_barrier((far, more_down))
        down_summed = lax.psum_scatter(more_down, "narrow", scatter_dimension=0, tiled=True)
        near.append(gather_halves(far, kept[:1], sizes, line[:1]))
        inner = [kept[1 : len(wide_bits)] for kept in flags]
        moved = pairs // 3
        near_cols = near[0].shape[1] - moved * PAIR
        near = [near[0][:, :near_cols], jnp.concatenate([near[1], near[0][:, near_cols:]], 1)]
        def finish(first_summed, hidden_summed, returned):
            return (
                finish_experts(first_summed, hidden_summed, 0),
                combine_out(returned, target, gate, resid),
            )

        *near, (hidden_grad, block_out) = gather_plane(
            *near, inner[0], sizes, plane, finish, (first_summed, hidden_summed, returned)
        )
        down_grad = finish_experts(first_summed, down_summed, 1)
        halves = [(half, swap(half)) for half in near]
        query_grad, key_grad, value_grad, output_weight_grad, centroids_grad, *vectors = spread(
            flag.reshape(1), halves, width, counts[0], moved, experts_all
        )
        centroids_grad = centroids_grad.T
        second_gain_grad, second_shift_grad, first_gain_grad, first_shift_grad = vectors
        return (
            block_out,
            input_grad,
            first_gain_grad,
            first_shift_grad,
            query_grad,
            key_grad,
            value_grad,
            output_weight_grad,
            second_gain_grad,
            second_shift_grad,
            centroids_grad,
            hidden_grad,
            down_grad,
        )

    return shards


def solution(mesh):
    tokens_spec = P(("wide", "narrow"), None, None)
    in_specs = (
        tokens_spec,
        P(("wide", "narrow")),
        tokens_spec,
        *[P()] * 9,
        P("wide", None, "narrow"),
        P("wide", "narrow", None),
        tokens_spec,
    )
    out_specs = (
        tokens_spec,
        tokens_spec,
        *[P()] * 9,
        P("wide", None, "narrow"),
        P("wide", "narrow", None),
    )
    return jax.shard_map(
        make_shards(mesh.shape["wide"], mesh.shape["narrow"]),
        mesh=mesh,
        in_specs=in_specs,
        out_specs=out_specs,
        check_vma=False,
    )
```

```python
import functools
import jax
import jax.numpy as jnp
from jax import lax
from jax.experimental import pallas as pl
from jax.experimental.pallas import tpu as pltpu
from jax.sharding import PartitionSpec as P

F32 = jnp.float32
BF16 = jnp.bfloat16
HEADS = 12
EPSILON = 1e-05
MASKED_SCORE = -1000000000.0
PAIR = 128
QTILE = 256


def dot(left, right):
    return jnp.dot(left, right, preferred_element_type=F32)


def dot_tn(left, right):
    return lax.dot_general(left, right, (((0,), (0,)), ((), ())), preferred_element_type=F32)


def dot_nt(left, right):
    return lax.dot_general(left, right, (((1,), (1,)), ((), ())), preferred_element_type=F32)


def lanes_of(head, shape):
    lane = lax.broadcasted_iota(jnp.int32, shape, 1)
    return (lane >= head * (PAIR // 2)) & (lane < (head + 1) * (PAIR // 2))


def packed_rows(length, tile):
    return [sum(range(1, at + 1)) * tile for at in range(length // tile + 1)]


def attend_kernel(scale, len_ref, q_ref, k_ref, v_ref, mixed_ref, probs_ref):
    length = q_ref.shape[0]
    tile = min(QTILE, length)
    seq_len = len_ref[0]
    starts = packed_rows(length, tile)
    for at in range(length // tile):
        start, finish = at * tile, (at + 1) * tile
        query = q_ref[start:finish, :] * scale
        keys = k_ref[:finish, :]
        values = v_ref[:finish, :]
        key_pos = lax.broadcasted_iota(jnp.int32, (finish, 1), 0)
        bias = jnp.where(key_pos < seq_len, 0.0, MASKED_SCORE)
        row = lax.broadcasted_iota(jnp.int32, (tile, tile), 0)
        col = lax.broadcasted_iota(jnp.int32, (tile, tile), 1)
        mixed = None
        for head in range(2):
            zero = jnp.zeros((), BF16)
            q_head = jnp.where(lanes_of(head, query.shape), query, zero)
            scores = dot_nt(keys, q_head) + bias
            diagonal = jnp.where(row <= col, scores[start:], MASKED_SCORE)
            scores = diagonal if start == 0 else jnp.concatenate([scores[:start], diagonal], 0)
            expo = jnp.exp(scores - jnp.max(scores, 0, keepdims=True))
            probs = (expo * (1.0 / jnp.sum(expo, 0, keepdims=True))).astype(BF16)
            probs_ref[0, head, starts[at] : starts[at + 1], :] = probs
            v_head = jnp.where(lanes_of(head, values.shape), values, zero)
            part = dot_tn(probs, v_head)
            mixed = part if mixed is None else mixed + part
        mixed_ref[start:finish, :] = mixed.astype(BF16)


def attend(projected, seq_lengths, scale):
    length, width3 = projected.shape
    width = width3 // 3
    pairs = width // PAIR
    tile = min(QTILE, length)
    rows = packed_rows(length, tile)[-1]
    return pl.pallas_call(
        functools.partial(attend_kernel, scale),
        grid_spec=pltpu.PrefetchScalarGridSpec(
            num_scalar_prefetch=1,
            grid=(pairs,),
            in_specs=[
                pl.BlockSpec((length, PAIR), lambda i, s: (0, i)),
                pl.BlockSpec((length, PAIR), lambda i, s: (0, pairs + i)),
                pl.BlockSpec((length, PAIR), lambda i, s: (0, 2 * pairs + i)),
            ],
            out_specs=[
                pl.BlockSpec((length, PAIR), lambda i, s: (0, i)),
                pl.BlockSpec((1, 2, rows, tile), lambda i, s: (i, 0, 0, 0)),
            ],
        ),
        out_shape=[
            jax.ShapeDtypeStruct((length, width), BF16),
            jax.ShapeDtypeStruct((pairs, 2, rows, tile), BF16),
        ],
        compiler_params=pltpu.CompilerParams(vmem_limit_bytes=48 * 1024 * 1024),
        cost_estimate=pl.CostEstimate(
            flops=4 * length * length * width, bytes_accessed=8 * length * width, transcendentals=0
        ),
        name="attend",
    )(seq_lengths, projected, projected, projected)


def attend_back_kernel(
    scale, counts, part, flag_ref, q_ref, k_ref, v_ref, g_ref, probs_ref, normed_t, *refs
):
    parts = len(counts)
    count = counts[part]
    last = part == parts - 1
    if part == 0:
        mixed_t, attn_ref, mine_ref, theirs_ref, grads = refs
    elif last:
        befores, refs = refs[: parts - 1], refs[parts - 1 :]
        qkv, (in_ref, gain_ref, resid_ref, cent_ref, sums_ref) = refs[:3], refs[3:8]
        mine_ref, theirs_ref, out_ref, grads, sums_scratch = refs[10:]
    else:
        mine_ref, theirs_ref, grads = refs
    length = q_ref.shape[0]
    tile = min(QTILE, length)
    starts = packed_rows(length, tile)
    step = pl.program_id(0)
    half = mine_ref.shape[0]
    columns = 3 * PAIR

    def give(product):
        low, high = product[:half], product[half:]
        mine_ref[...] = jnp.where(flag_ref[0] == 0, low, high)
        theirs_ref[...] = jnp.where(flag_ref[0] == 0, high, low).astype(BF16)

    def pair():
        dk_sum = [None] * (length // tile)
        dv_sum = [None] * (length // tile)
        dq = []
        for at in range(length // tile):
            start, finish = at * tile, (at + 1) * tile
            query = q_ref[start:finish, :] * scale
            grad = g_ref[start:finish, :]
            keys = k_ref[:finish, :]
            values = v_ref[:finish, :]
            grad_query = None
            for head in range(2):
                zero = jnp.zeros((), BF16)
                q_head = jnp.where(lanes_of(head, query.shape), query, zero)
                g_head = jnp.where(lanes_of(head, query.shape), grad, zero)
                k_head = jnp.where(lanes_of(head, keys.shape), keys, zero)
                low = probs_ref[0, head, starts[at] : starts[at + 1], :]
                probs = low.astype(F32)
                product = probs * dot_nt(values, g_head)
                centre = jnp.sum(product, 0, keepdims=True)
                grad_scores = (product - probs * centre).astype(BF16)
                dv = dot(low, g_head)
                dk = dot(grad_scores, q_head)
                for j in range(at + 1):
                    here = slice(j * tile, (j + 1) * tile)
                    dk_sum[j] = dk[here] if dk_sum[j] is None else dk_sum[j] + dk[here]
                    dv_sum[j] = dv[here] if dv_sum[j] is None else dv_sum[j] + dv[here]
                share = dot_tn(grad_scores, k_head)
                grad_query = share if grad_query is None else grad_query + share
            dq.append((grad_query * scale).astype(BF16))
        sides = [dq, [x.astype(BF16) for x in dk_sum], [x.astype(BF16) for x in dv_sum]]
        return jnp.concatenate([jnp.concatenate(side, 0) for side in sides], 1)

    @pl.when(step < count)
    def _():
        found = pair()
        for k in range(3):
            cols = pl.ds(pl.multiple_of(step * PAIR, PAIR), PAIR) if last else slice(None)
            grads[k, :, cols] = found[:, k * PAIR : (k + 1) * PAIR]
        give(dot(normed_t[...], found))

    if part == 0:

        @pl.when(step >= count)
        def _():
            give(dot(mixed_t[...], attn_ref[...]))

    if last:

        @pl.when(step == count)
        def _():
            sums_scratch[...] = jnp.zeros_like(sums_scratch)

        @pl.when(step >= count)
        def _():
            here = pl.ds(pl.multiple_of((step - count) * tile, tile), tile)
            grad = None
            for j in range(parts):
                before = sum(counts[:j])
                cols = slice(before * PAIR, (before + counts[j]) * PAIR)
                for k, weight in enumerate(qkv):
                    side = grads[k, here, :] if j == parts - 1 else befores[j][k]
                    share = dot_nt(side, weight[:, cols])
                    grad = share if grad is None else grad + share
            standard, back_norm = norm_back(in_ref[0].astype(F32), gain_ref[...], grad)
            out_ref[0] = (resid_ref[...] + back_norm).astype(BF16)
            sums_scratch[0:1, :] += jnp.sum(grad * standard, 0, keepdims=True)
            sums_scratch[1:2, :] += jnp.sum(grad, 0, keepdims=True)

        @pl.when(step == count + length // tile - 1)
        def _():
            sums = cent_ref[...]
            rows, width = sums.shape
            place = lax.broadcasted_iota(jnp.int32, (rows, 1), 0)
            for row, ref, k in (
                (rows - 4, sums_ref, 0), (rows - 3, sums_ref, 1),
                (rows - 2, sums_scratch, 0), (rows - 1, sums_scratch, 1),
            ):
                sums = jnp.where(place == row, ref[k : k + 1, :], sums)
            turned = jnp.concatenate([sums, jnp.zeros((PAIR - rows, width), F32)], 0).T
            low, high = turned[:half], turned[half:]
            mine_ref[:, :PAIR] = jnp.where(flag_ref[0] == 0, low, high)
            theirs_ref[:, :PAIR] = jnp.where(flag_ref[0] == 0, high, low).astype(BF16)


def attend_back(flag, projected, grad_mixed, probs, scale, counts, part, normed_t, *more):
    width, length = normed_t.shape
    pairs = width // PAIR
    count = counts[part]
    first = sum(counts[:part])
    last = part == len(counts) - 1
    block = (length, PAIR)
    columns = 3 * PAIR
    extra = width // columns if part == 0 else 0

    def at(i):
        return first + jnp.minimum(i, count - 1)

    own = (count + extra) * columns
    held = own if part == 0 else sum(counts[1:]) * columns + PAIR
    offset = sum(counts[1:part])
    steps = count + (1 if last else extra)
    half_spec = pl.BlockSpec(
        (width // 2, columns), lambda i, s: (0, offset + jnp.minimum(i, steps - 1))
    )
    half_shape = (width // 2, held)
    in_specs = [
        pl.BlockSpec(block, lambda i, s: (0, at(i))),
        pl.BlockSpec(block, lambda i, s: (0, pairs + at(i))),
        pl.BlockSpec(block, lambda i, s: (0, 2 * pairs + at(i))),
        pl.BlockSpec(block, lambda i, s: (0, at(i))),
        pl.BlockSpec((1, *probs.shape[1:]), lambda i, s: (at(i), 0, 0, 0)),
        whole(normed_t.shape),
    ]
    out_specs = [half_spec, half_spec]
    out_shape = [jax.ShapeDtypeStruct(half_shape, F32), jax.ShapeDtypeStruct(half_shape, BF16)]
    scratch = []
    aliases = {}
    if last:
        tile = min(QTILE, length)

        def row(i):
            return jnp.maximum(i - count, 0)

        in_specs += [
            pl.BlockSpec((3, tile, c * PAIR), lambda i, s: (0, row(i), 0)) for c in counts[:-1]
        ]
        in_specs += [whole((width, width))] * 3
        in_specs += [
            pl.BlockSpec((1, tile, width), lambda i, s: (0, row(i), 0)), whole((1, width)),
            pl.BlockSpec((tile, width), lambda i, s: (row(i), 0)), whole(more[-4].shape),
            whole(more[-3].shape),
        ]
        in_specs += [pl.BlockSpec(memory_space=pl.ANY)] * 2
        aliases = {5 + len(more): 0, 6 + len(more): 1}
        extra = length // tile
        out_specs += [pl.BlockSpec((1, tile, width), lambda i, s: (0, row(i), 0))]
        out_shape += [jax.ShapeDtypeStruct((1, length, width), BF16)]
        scratch += [pltpu.VMEM((3, length, count * PAIR), BF16), pltpu.VMEM((8, width), F32)]
    else:
        if part == 0:
            in_specs += [
                whole((width, length)),
                pl.BlockSpec((length, columns), lambda i, s: (0, jnp.maximum(i - count, 0))),
            ]
        out_specs += [
            pl.BlockSpec((3, length, PAIR), lambda i, s: (0, 0, jnp.minimum(i, count - 1)))
        ]
        out_shape += [jax.ShapeDtypeStruct((3, length, count * PAIR), BF16)]
    return pl.pallas_call(
        functools.partial(attend_back_kernel, scale, counts, part),
        grid_spec=pltpu.PrefetchScalarGridSpec(
            num_scalar_prefetch=1,
            grid=(count + extra,),
            in_specs=in_specs,
            out_specs=out_specs,
            scratch_shapes=scratch,
        ),
        out_shape=out_shape,
        input_output_aliases=aliases,
        compiler_params=pltpu.CompilerParams(vmem_limit_bytes=58 * 1024 * 1024),
        cost_estimate=pl.CostEstimate(
            flops=20 * length * length * count * PAIR,
            bytes_accessed=14 * length * count * PAIR,
            transcendentals=0,
        ),
        name="attend_back",
    )(flag, projected, projected, projected, grad_mixed, probs, normed_t, *more)


ERFC = (0.254829592, -0.284496736, 1.421413741, -1.453152027, 1.061405429)
ERFC_RATE = 0.3275911 * 0.5**0.5
ROWS = 256


def gelu_pair(value):
    size = jnp.abs(value)
    t = 1.0 / (1.0 + ERFC_RATE * size)
    poly = t * (
        ERFC[0] + t * (ERFC[1] + t * (ERFC[2] + t * (ERFC[3] + t * ERFC[4])))
    )
    bell = jnp.exp(-0.5 * value * value)
    tail = 0.5 * poly * bell
    below = jnp.where(value < 0, tail, 1.0 - tail)
    return value * below, below + value * (bell * 0.3989422804014327)


def join_pieces(w_ref, w_all):
    pieces, unused, hidden, unused_width = w_ref.shape
    for p in range(pieces):
        for k in range(2):
            w_all[k, p * hidden : (p + 1) * hidden, :] = w_ref[p, k]


def expert_tile(x, g, w_all, active_ref, pre_ref, at):
    units = w_all.shape[1]
    chunk = units if units <= 512 else 512 if units % 512 == 0 else 384
    for start in range(0, units, chunk):
        cols = slice(start, start + chunk)
        active, slope = gelu_pair(dot_nt(x, w_all[0, cols, :]))
        active_ref[at, cols] = active.astype(BF16)
        pre_ref[at, cols] = (dot_nt(g, w_all[1, cols, :]) * slope).astype(BF16)
    return dot(active_ref[at, :], w_all[1]), dot(pre_ref[at, :], w_all[0])


def expert_first_kernel(
    tiles, x_ref, u_ref, cent_ref, w_ref, out_ref, in_ref, dw_ref, g_ref, xt_ref, gt_ref, gate_ref,
    active, grad_pre, w_all,
):
    rows = x_ref.shape[0]
    step = pl.program_id(0)

    @pl.when(step == 0)
    def _():
        join_pieces(w_ref, w_all)

    @pl.when(step < tiles)
    def _():
        at = pl.ds(pl.multiple_of(step * rows, rows), rows)
        x = x_ref[...]
        chosen = jnp.sum(x.astype(F32) * cent_ref[...], 1, keepdims=True)
        gate = 1.0 / (1.0 + jnp.exp(-chosen))
        gate_ref[...] = gate
        g = (gate * u_ref[...].astype(F32)).astype(BF16)
        g_ref[...] = g
        xt_ref[:, at] = x.T
        gt_ref[:, at] = g.T
        out_ref[...], in_ref[...] = expert_tile(x, g, w_all, active, grad_pre, at)

    @pl.when(step >= tiles)
    def _():
        hidden = dw_ref.shape[3]
        cols = pl.ds(pl.multiple_of((step - tiles) * hidden, hidden), hidden)
        dw_ref[0, 0] = dot(xt_ref[...], grad_pre[:, cols]).astype(BF16)
        dw_ref[0, 1] = dot(gt_ref[...], active[:, cols]).astype(BF16)


def expert_last_kernel(
    x_ref, g_ref, u_ref, gate_ref, cent_ref, out_in, in_in, w_ref,
    low_ref, back_ref, cent_grad_ref, active_ref, pre_ref, w_all,
):
    @pl.when(pl.program_id(0) == 0)
    def _():
        join_pieces(w_ref, w_all)
        cent_grad_ref[...] = jnp.zeros_like(cent_grad_ref)

    x = x_ref[...]
    out, grad_in = expert_tile(x, g_ref[...], w_all, active_ref, pre_ref, slice(None))
    low = (out_in[...] + out).astype(BF16)
    low_ref[...] = low
    gate = gate_ref[...]
    chosen = jnp.sum(u_ref[...].astype(F32) * low.astype(F32), 1, keepdims=True)
    chosen = chosen * gate * (1.0 - gate)
    back_ref[...] = (in_in[...] + grad_in + chosen * cent_ref[...]).astype(BF16)
    cent_grad_ref[...] += jnp.sum(chosen * x.astype(F32), 0, keepdims=True)


def expert_weights_kernel(xt_ref, gt_ref, active_ref, pre_ref, hidden_ref, down_ref):
    hidden_ref[0] = dot(xt_ref[...], pre_ref[...]).astype(BF16)
    down_ref[0] = dot(gt_ref[...], active_ref[...]).astype(BF16)


def whole(shape):
    return pl.BlockSpec(shape, lambda *i: (0,) * len(shape), pipeline_mode=pl.Buffered(1))


EXPERT_PARAMS = pltpu.CompilerParams(vmem_limit_bytes=58 * 1024 * 1024)


def expert_cost(kind, rows, width, hidden, pieces):
    return pl.CostEstimate(
        flops=2 * kind * rows * width * hidden * pieces,
        bytes_accessed=6 * rows * width * 4,
        transcendentals=0,
    )


def expert_first(x, u, cent, w):
    rows, width = x.shape
    pieces, unused, hidden, unused_width = w.shape
    tile = min(ROWS, rows)
    tiles = rows // tile
    units = pieces * hidden

    def tiled(cols):
        return pl.BlockSpec((tile, cols), lambda i: (jnp.minimum(i, tiles - 1), 0))

    wide = jax.ShapeDtypeStruct((rows, width), F32)
    turned = jax.ShapeDtypeStruct((width, rows), BF16)
    return pl.pallas_call(
        functools.partial(expert_first_kernel, tiles),
        grid=(tiles + pieces,),
        in_specs=[tiled(width), tiled(width), whole((1, width)), whole(w.shape)],
        out_specs=[
            tiled(width), tiled(width),
            pl.BlockSpec((1, 2, width, hidden), lambda i: (jnp.maximum(i - tiles, 0), 0, 0, 0)),
            tiled(width), whole(turned.shape), whole(turned.shape), tiled(1),
        ],
        out_shape=[
            wide, wide, jax.ShapeDtypeStruct((pieces, 2, width, hidden), BF16),
            jax.ShapeDtypeStruct((rows, width), BF16), turned, turned,
            jax.ShapeDtypeStruct((rows, 1), F32),
        ],
        scratch_shapes=[
            pltpu.VMEM((rows, units), BF16), pltpu.VMEM((rows, units), BF16),
            pltpu.VMEM((2, units, width), BF16),
        ],
        compiler_params=EXPERT_PARAMS,
        cost_estimate=expert_cost(6, rows, width, hidden, pieces),
        name="expert_first",
    )(x, u, cent, w)


def expert_last(x, g, u, gate, cent, out_sum, in_sum, w):
    rows, width = x.shape
    pieces, unused, hidden, unused_width = w.shape
    tile = min(ROWS, rows)
    units = pieces * hidden

    def tiled(cols):
        return pl.BlockSpec((tile, cols), lambda i: (i, 0))

    low = jax.ShapeDtypeStruct((rows, width), BF16)
    kept = jax.ShapeDtypeStruct((rows, units), BF16)
    return pl.pallas_call(
        expert_last_kernel,
        grid=(rows // tile,),
        in_specs=[tiled(width)] * 3
        + [tiled(1), whole((1, width)), tiled(width), tiled(width), whole(w.shape)],
        out_specs=[tiled(width), tiled(width), whole((1, width)), tiled(units), tiled(units)],
        out_shape=[low, low, jax.ShapeDtypeStruct((1, width), F32), kept, kept],
        scratch_shapes=[pltpu.VMEM((2, units, width), BF16)],
        compiler_params=EXPERT_PARAMS,
        cost_estimate=expert_cost(4, rows, width, hidden, pieces),
        name="expert_last",
    )(x, g, u, gate, cent, out_sum, in_sum, w)


def expert_weights(xt, gt, active, grad_pre, pieces):
    width, rows = xt.shape
    hidden = active.shape[1] // pieces
    kept_spec = pl.BlockSpec((rows, hidden), lambda i: (0, i))
    shape = (pieces, width, hidden)
    piece = pl.BlockSpec((1, width, hidden), lambda i: (i, 0, 0))
    return pl.pallas_call(
        expert_weights_kernel,
        grid=(pieces,),
        in_specs=[whole(xt.shape), whole(xt.shape), kept_spec, kept_spec],
        out_specs=[piece, piece],
        out_shape=[jax.ShapeDtypeStruct(shape, BF16)] * 2,
        compiler_params=EXPERT_PARAMS,
        cost_estimate=expert_cost(2, rows, width, hidden, pieces),
        name="expert_weights",
    )(xt, gt, active, grad_pre)


def norm_back(values, gain, grad):
    centre = jnp.mean(values, -1, keepdims=True)
    centered = values - centre
    spread = jnp.mean(centered * centered, -1, keepdims=True)
    rate = lax.rsqrt(spread + EPSILON)
    standard = centered * rate
    u = grad * gain
    back = rate * (
        u - jnp.mean(u, -1, keepdims=True) - standard * jnp.mean(u * standard, -1, keepdims=True)
    )
    return standard, back


def combine_back_kernel(
    back_ref, target_ref, resid_ref, cot_ref, gain_ref, weight_ref,
    resid_grad_ref, attn_ref, mixed_grad_ref, sums_ref,
):
    @pl.when(pl.program_id(0) == 0)
    def _():
        sums_ref[...] = jnp.zeros_like(sums_ref)

    target = target_ref[...]
    slots = lax.broadcasted_iota(jnp.int32, (1, back_ref.shape[0]), 1)
    grad = dot((target == slots).astype(BF16), back_ref[...])
    standard, back_norm = norm_back(resid_ref[...], gain_ref[...], grad)
    upstream = jnp.where(target >= 0, cot_ref[...].astype(F32), 0.0)
    grad_resid = upstream + back_norm
    resid_grad_ref[...] = grad_resid
    low = grad_resid.astype(BF16)
    attn_ref[...] = low
    mixed_grad_ref[...] = dot_nt(low, weight_ref[...]).astype(BF16)
    sums_ref[0:1, :] += jnp.sum(grad * standard, 0, keepdims=True)
    sums_ref[1:2, :] += jnp.sum(grad, 0, keepdims=True)


def combine_back(back, target, resid, cot, gain, weight):
    length, width = resid.shape
    tile = min(QTILE, length)
    tiled = pl.BlockSpec((tile, width), lambda i: (i, 0))
    low = jax.ShapeDtypeStruct(resid.shape, BF16)
    return pl.pallas_call(
        combine_back_kernel,
        grid=(length // tile,),
        in_specs=[
            whole(back.shape), pl.BlockSpec((tile, 1), lambda i: (i, 0)), tiled, tiled,
            whole((1, width)), whole(weight.shape),
        ],
        out_specs=[tiled, tiled, tiled, whole((8, width))],
        out_shape=[
            jax.ShapeDtypeStruct(resid.shape, F32), low, low, jax.ShapeDtypeStruct((8, width), F32),
        ],
        compiler_params=EXPERT_PARAMS,
        cost_estimate=pl.CostEstimate(
            flops=2 * length * width * (back.shape[0] + width),
            bytes_accessed=20 * length * width,
            transcendentals=0,
        ),
        name="combine_back",
    )(back, target, resid, cot, gain.reshape(1, width), weight)


def combine_out_kernel(rows_ref, target_ref, gate_ref, resid_ref, out_ref):
    slots = lax.broadcasted_iota(jnp.int32, (1, rows_ref.shape[0]), 1)
    rows = dot((target_ref[...] == slots).astype(BF16), rows_ref[...])
    out_ref[0] = (resid_ref[...] + gate_ref[...] * rows).astype(BF16)


def combine_out(rows, target, gate, resid):
    length, width = resid.shape
    tile = min(2 * QTILE, length)
    column = pl.BlockSpec((tile, 1), lambda i: (i, 0))
    return pl.pallas_call(
        combine_out_kernel,
        grid=(length // tile,),
        in_specs=[
            whole(rows.shape), column, column, pl.BlockSpec((tile, width), lambda i: (i, 0)),
        ],
        out_specs=pl.BlockSpec((1, tile, width), lambda i: (0, i, 0)),
        out_shape=jax.ShapeDtypeStruct((1, length, width), BF16),
        compiler_params=EXPERT_PARAMS,
        cost_estimate=pl.CostEstimate(flops=1, bytes_accessed=1, transcendentals=0),
        name="combine_out",
    )(rows, target, gate, resid)


def finish_hidden_kernel(blocks, first_ref, second_ref, out_ref):
    step = pl.program_id(0)

    @pl.when(step < blocks)
    def _():
        out_ref[0] = first_ref[0, 0].astype(F32)

    @pl.when(step >= blocks)
    def _():
        out_ref[0] = second_ref[0].astype(F32)


def finish_hidden(first, second):
    unused, width, size = second.shape
    blocks = first.shape[3] // size
    return pl.pallas_call(
        functools.partial(finish_hidden_kernel, blocks),
        grid=(blocks + 1,),
        in_specs=[
            pl.BlockSpec((1, 1, width, size), lambda i: (0, 0, 0, jnp.minimum(i, blocks - 1))),
            whole(second.shape),
        ],
        out_specs=pl.BlockSpec((1, width, size), lambda i: (0, 0, i)),
        out_shape=jax.ShapeDtypeStruct((1, width, (blocks + 1) * size), F32),
        compiler_params=EXPERT_PARAMS,
        name="finish_hidden",
    )(first, second)


def finish_down_kernel(rows_ref, *refs):
    refs[-1][0] = rows_ref[...].reshape(rows_ref.shape[-2:]).T.astype(F32)


def finish_down(source, size, blocks, filled=None):
    width = source.shape[-2]
    if filled is None:
        specs = [pl.BlockSpec((1, 1, width, size), lambda i: (0, 1, 0, i))]
        operands, steps, at = (source,), blocks, 0
    else:
        specs = [whole(source.shape), pl.BlockSpec(memory_space=pl.ANY)]
        operands, steps, at = (source, filled), 1, blocks
    return pl.pallas_call(
        finish_down_kernel,
        grid=(steps,),
        in_specs=specs,
        out_specs=pl.BlockSpec((1, size, width), lambda i: (0, at + i, 0)),
        out_shape=jax.ShapeDtypeStruct((1, (blocks + 1) * size, width), F32),
        input_output_aliases={} if filled is None else {1: 0},
        compiler_params=EXPERT_PARAMS,
        name="finish_down",
    )(*operands)


def spread_kernel(
    near, moved, flag_ref, one_ref, one_other, two_ref, two_other,
    query_ref, key_ref, value_ref, output_ref, cent_ref, *vectors,
):
    step = pl.program_id(0)
    steps = pl.num_programs(0)
    half = query_ref.shape[0] // 2
    chains = ((one_ref, one_other), (two_ref, two_other))

    def halves(chain, block):
        cols = pl.ds(pl.multiple_of(block * PAIR, PAIR), PAIR)
        low, high = [side[:, cols].astype(F32) for side in chains[chain]]
        return jnp.where(flag_ref[0] == 0, low, high), jnp.where(flag_ref[0] == 0, high, low)

    for k, here in enumerate((step < near, step >= near)):

        @pl.when(here)
        def _():
            for i, at in enumerate((query_ref, key_ref, value_ref)):
                at[:half, :], at[half:, :] = halves(k, 3 * (step - near * k) + i)

    kept = steps - moved
    sums_at = 3 * (steps - near)
    for k, here in enumerate((step < kept, step >= kept)):

        @pl.when(here)
        def _():
            block = sums_at + 1 + step - kept if k else 3 * near + step
            output_ref[:half, :], output_ref[half:, :] = halves(k, block)

    @pl.when(step == 0)
    def _():
        side = jnp.concatenate([x.T for x in halves(1, sums_at)], 1)
        experts = cent_ref.shape[0]
        cent_ref[...] = side[:experts]
        for ref, row in vectors_of(vectors, experts):
            ref[...] = side[row]


def vectors_of(refs, experts):
    last = experts + 4 + -(experts + 4) % 8
    return zip(refs, range(last - 4, last))


def spread(flag, halves, width, near, moved, experts):
    pairs = width // PAIR
    out = jax.ShapeDtypeStruct((width, width), F32)
    vector = jax.ShapeDtypeStruct((width,), F32)
    return pl.pallas_call(
        functools.partial(spread_kernel, near, moved),
        grid=(pairs,),
        in_specs=[pl.BlockSpec(memory_space=pltpu.SMEM)]
        + [pl.BlockSpec(memory_space=pltpu.VMEM)] * 4,
        out_specs=[pl.BlockSpec((width, PAIR), lambda i: (0, i))] * 4
        + [whole((experts, width))]
        + [whole((width,))] * 4,
        out_shape=[out] * 4 + [jax.ShapeDtypeStruct((experts, width), F32)] + [vector] * 4,
        compiler_params=pltpu.CompilerParams(vmem_limit_bytes=32 * 1024 * 1024),
        name="spread",
    )(flag, *halves[0], *halves[1])


def normalize(values, gain, shift):
    centre = jnp.mean(values, -1, keepdims=True)
    centered = values - centre
    spread = jnp.mean(centered * centered, -1, keepdims=True)
    return centered * lax.rsqrt(spread + EPSILON) * gain + shift


def xor_pairs(size, flip):
    return [(i, i ^ flip) for i in range(size)]


def exchange(rows, blocks):
    shape = rows.shape
    return lax.all_to_all(
        rows.reshape(blocks, -1, shape[1]), "wide", split_axis=0, concat_axis=0, tiled=True
    ).reshape(shape)


def add_up(terms):
    return functools.reduce(lambda a, b: a + b, [t.astype(F32) for t in terms])


def reduce_halves(terms, flags, sizes, bits, beside=None):
    for i, (axis, flip) in enumerate(bits):
        flag = (lax.axis_index(axis) // flip) % 2
        half = terms[0].shape[0] // 2
        mine, theirs = [
            [lax.dynamic_slice_in_dim(t, f * half, half, 0) for t in terms] for f in (flag, 1 - flag)
        ]
        came = lax.ppermute(add_up(theirs).astype(BF16), axis, xor_pairs(sizes[axis], flip))
        if beside is not None and i == len(bits) - 1:
            came, *beside = lax.optimization_barrier((came, *beside))
        terms = [add_up([*mine, came])]
        flags.append(flag)
    return terms[0] if beside is None else (terms[0], *beside)


def gather_halves(total, flags, sizes, bits):
    for at in reversed(range(len(bits))):
        axis, flip = bits[at]
        other = lax.ppermute(total, axis, xor_pairs(sizes[axis], flip))
        total = jnp.where(
            flags[at] == 0, jnp.concatenate([total, other], 0), jnp.concatenate([other, total], 0)
        )
    return total


def gather_plane(one, two, flags, sizes, bits, works):
    columns = two.shape[1]
    found = []
    for at, (axis, flip) in enumerate(bits):
        back = len(bits) - 1 - at
        beside = None
        if at in works:
            work, operands = works[at]
            one, two, operands = lax.optimization_barrier((one, two, operands))
            beside = work(*operands)
        came = [
            lax.ppermute(one, bits[back][0], xor_pairs(sizes[bits[back][0]], bits[back][1])),
            lax.ppermute(two, axis, xor_pairs(sizes[axis], flip)),
        ]
        if beside is not None:
            came, beside = lax.optimization_barrier((came, beside))
            found.append(beside)
        came_one, came_two = lax.optimization_barrier(came)
        one = jnp.where(
            flags[back] == 0, jnp.concatenate([one, came_one], 0), jnp.concatenate([came_one, one], 0)
        )
        two = jnp.where(
            flags[at] == 0, jnp.stack([two, came_two], at), jnp.stack([came_two, two], at)
        )
    return one, two.reshape(-1, columns), *found


def make_shards(n_wide, n_narrow):
    sizes = {"wide": n_wide, "narrow": n_narrow}
    wide_bits = [("wide", 1 << i) for i in range(n_wide.bit_length() - 1)]
    narrow_bits = [("narrow", 1 << i) for i in range(n_narrow.bit_length() - 1)]

    def shards(
        block_in,
        seq_lengths,
        routes,
        first_gain,
        first_shift,
        query_weight,
        key_weight,
        value_weight,
        output_weight,
        second_gain,
        second_shift,
        centroids,
        hidden_weight,
        down_weight,
        cotangent,
    ):
        seqs_here, length, width = block_in.shape
        head_size = width // HEADS
        scale = head_size ** (-0.5)
        tokens = seqs_here * length
        experts_all = centroids.shape[1]
        capacity = 3 * tokens // (2 * experts_all)
        wide_here = lax.axis_index("wide")
        hidden_size = hidden_weight.shape[2]

        second = max(hidden_size // 3 // 128 * 128, 128)
        cuts = (0, hidden_size - second, hidden_size)
        hidden_t = hidden_weight[0].T
        packs = [
            jnp.stack([hidden_t[a:b], down_weight[0, a:b]], 0)[None]
            for a, b in zip(cuts, cuts[1:])
        ]
        packs[0], block_in, seq_lengths, routes, cotangent = lax.optimization_barrier(
            (packs[0], block_in, seq_lengths, routes, cotangent)
        )
        weights = [lax.all_gather(pack, "narrow", axis=0, tiled=True) for pack in packs]

        live = lax.broadcasted_iota(jnp.int32, (tokens,), 0) < seq_lengths[0]
        route = routes.reshape(tokens)
        expert_ids = lax.broadcasted_iota(jnp.int32, (tokens, experts_all), 1)
        picked = route[:, None] == expert_ids
        ones_live = (picked & live[:, None]).astype(jnp.int32)
        earlier = jnp.cumsum(ones_live, 0, dtype=jnp.int32) - ones_live
        slot = jnp.sum(earlier * ones_live, 1, dtype=jnp.int32)
        target = route * capacity + slot
        slot_ids = lax.broadcasted_iota(jnp.int32, (tokens, experts_all * capacity), 1)
        target = jnp.where(live, target, -1)[:, None]
        table = (target == slot_ids).astype(BF16)
        cot = cotangent.reshape(tokens, width)

        def to_slots(rows):
            return dot_tn(table, rows).astype(BF16)

        upstream_slots, block_in, *packs = lax.optimization_barrier(
            (to_slots(cot), block_in, *packs)
        )
        upstream_rows = exchange(upstream_slots, experts_all)

        qkv_weight = jnp.concatenate([query_weight, key_weight, value_weight], 1)
        inputs_wide = block_in.reshape(tokens, width).astype(F32)
        normed_low = normalize(inputs_wide, first_gain, first_shift).astype(BF16)
        projected = dot(normed_low, qkv_weight).astype(BF16)
        mixed, probs = attend(projected, seq_lengths, scale)
        mixed, upstream_rows = lax.optimization_barrier((mixed, upstream_rows))
        resid = inputs_wide + dot(mixed, output_weight)
        normed_second = normalize(resid, second_gain, second_shift).astype(BF16)

        pairs = width // PAIR
        counts = (pairs // 2, pairs // 3, pairs - pairs // 2 - pairs // 3)
        logits = dot(normed_second, centroids)
        gate = jax.nn.sigmoid(jnp.sum(jnp.where(picked, logits, 0.0), 1, keepdims=True))
        slots, normed_t, mixed_t, gate, target = lax.optimization_barrier(
            (to_slots(normed_second), normed_low.T, mixed.T, gate, target)
        )
        rows = exchange(slots, experts_all)
        own_centroid = lax.dynamic_slice_in_dim(centroids.T, wide_here, 1, 0).astype(F32)
        out_sum, in_sum, weight_grads, grad_rows, rows_t, grad_rows_t, row_gate = expert_first(
            rows, upstream_rows, own_centroid, weights[0]
        )
        out_low, back_rows, own_centroid_grad, *kept = expert_last(
            rows, grad_rows, upstream_rows, row_gate, own_centroid, out_sum, in_sum, weights[1]
        )
        back = exchange(back_rows, experts_all)
        more_hidden, more_down = expert_weights(rows_t, grad_rows_t, *kept, n_narrow)
        own_row = lax.broadcasted_iota(jnp.int32, (experts_all + 4 + -(experts_all + 4) % 8, 1), 0)
        sums = jnp.where(own_row == wide_here, own_centroid_grad, 0.0)
        sums, back = lax.optimization_barrier((sums, back))
        grad_resid, grad_attn, grad_mixed, second_sums = combine_back(
            back, target, resid, cot, second_gain, output_weight
        )
        out_low, more_hidden, more_down, grad_mixed = lax.optimization_barrier(
            (out_low, more_hidden, more_down, grad_mixed)
        )
        returned = exchange(out_low, experts_all)

        flag = wide_here % 2
        shared = (flag.reshape(1), projected, grad_mixed, probs, scale)
        core, plane, line = wide_bits[:1], wide_bits[1:], narrow_bits
        flags = [[flag], [flag]]

        def swap(half):
            return lax.ppermute(half, "wide", xor_pairs(n_wide, 1))

        first_summed = lax.psum_scatter(weight_grads, "narrow", scatter_dimension=0, tiled=True)
        mine_one, theirs_one, grads_one = attend_back(
            *shared, counts, 0, normed_t, mixed_t, grad_attn
        )
        came_one = swap(theirs_one)
        mine_two, theirs_two, grads_two = attend_back(*shared, counts, 1, normed_t)
        grads_two, returned, came_one, more_hidden = lax.optimization_barrier(
            (grads_two, returned, came_one, more_hidden)
        )
        hidden_summed = lax.psum_scatter(more_hidden, "narrow", scatter_dimension=0, tiled=True)
        mine_two, theirs_two, input_grad = attend_back(
            *shared, counts, 2, normed_t, grads_one, grads_two, query_weight, key_weight, value_weight, block_in,
            first_gain.reshape(1, width), grad_resid, sums, second_sums, mine_two, theirs_two,
        )
        chain_one, mine_two, theirs_two, first_summed = reduce_halves(
            [mine_one, came_one], flags[0], sizes, plane[:1], (mine_two, theirs_two, first_summed)
        )
        chain_two = [mine_two, swap(theirs_two)]
        chain_one = reduce_halves([chain_one], flags[0], sizes, plane[1:] + line)
        chain_two = reduce_halves(chain_two, flags[1], sizes, plane[:1])
        chain_two, hidden_summed = reduce_halves(
            [chain_two], flags[1], sizes, plane[1:], (hidden_summed,)
        )
        chain_two = reduce_halves([chain_two], flags[1], sizes, line)
        near = [
            gather_halves(total.astype(BF16), kept[-len(line) :], sizes, line)
            for total, kept in ((chain_one, flags[0]),)
        ]
        kept = flags[1][-len(line) :]
        far = gather_halves(chain_two.astype(BF16), kept[1:], sizes, line[1:])
        far, more_down = lax.optimization_barrier((far, more_down))
        down_summed = lax.psum_scatter(more_down, "narrow", scatter_dimension=0, tiled=True)
        near.append(gather_halves(far, kept[:1], sizes, line[:1]))
        inner = [kept[1 : len(wide_bits)] for kept in flags]
        moved = pairs // 3
        near_cols = near[0].shape[1] - moved * PAIR
        near = [near[0][:, :near_cols], jnp.concatenate([near[1], near[0][:, near_cols:]], 1)]
        size = down_summed.shape[2]
        blocks = first_summed.shape[3] // size

        def finish_early(first_summed, hidden_summed):
            return finish_hidden(first_summed, hidden_summed), finish_down(first_summed, size, blocks)

        works = {
            0: (finish_early, (first_summed, hidden_summed)),
            len(plane) - 1: (combine_out, (returned, target, gate, resid)),
        }
        *near, (hidden_grad, down_grad), block_out = gather_plane(
            *near, inner[0], sizes, plane, works
        )
        down_grad = finish_down(down_summed, size, blocks, down_grad)
        halves = [(half, swap(half)) for half in near]
        query_grad, key_grad, value_grad, output_weight_grad, centroids_grad, *vectors = spread(
            flag.reshape(1), halves, width, counts[0], moved, experts_all
        )
        centroids_grad = centroids_grad.T
        second_gain_grad, second_shift_grad, first_gain_grad, first_shift_grad = vectors
        return (
            block_out,
            input_grad,
            first_gain_grad,
            first_shift_grad,
            query_grad,
            key_grad,
            value_grad,
            output_weight_grad,
            second_gain_grad,
            second_shift_grad,
            centroids_grad,
            hidden_grad,
            down_grad,
        )

    return shards


def solution(mesh):
    tokens_spec = P(("wide", "narrow"), None, None)
    in_specs = (
        tokens_spec,
        P(("wide", "narrow")),
        tokens_spec,
        *[P()] * 9,
        P("wide", None, "narrow"),
        P("wide", "narrow", None),
        tokens_spec,
    )
    out_specs = (
        tokens_spec,
        tokens_spec,
        *[P()] * 9,
        P("wide", None, "narrow"),
        P("wide", "narrow", None),
    )
    return jax.shard_map(
        make_shards(mesh.shape["wide"], mesh.shape["narrow"]),
        mesh=mesh,
        in_specs=in_specs,
        out_specs=out_specs,
        check_vma=False,
    )
```
